256 devices in a mesh: group: 16 (over y, x_lo, core), fsdp: 16 (over x_hi, z).
Axes of the slice: x: 4 (x_hi: 2, x_lo: 2; x = x_hi * 2 + x_lo), y: 4, z: 8, core: 2. Of those that a mesh axis runs over, the one named last changes fastest.
Arguments:
- inputs: bfloat16 [16, 5120, 5120], P('group', 'fsdp'), may hold values from -6 to 6
- key_grad: bfloat16 [16, 5120, 1024], P('group', 'fsdp'), may hold values from -6 to 6
- seg_ids: int32 [16, 5120], P('group', 'fsdp'), may hold values from 0 to 15, never falling along the last dimension, each value on 1 to 2560 neighbouring positions
- advantages: float32 [16, 16], P('group'), may hold values from -4 to 4
- gains: bfloat16 [16, 5120], P('group', 'fsdp'), may hold values from 0.5 to 1.5
- local_weights: bfloat16 [16, 5120, 1024], P('group', 'fsdp'), may hold values from -6 to 6
- outer_weights: float32 [5120, 1024], P('fsdp'), may hold values from -6 to 6
- momentum: float32 [5120, 1024], P('fsdp'), may hold values from -3 to 3
- frag_index: int32 [1], replicated, may hold values from 0 to 3
Outputs:
- keys: bfloat16 [16, 5120, 1024], P('group', 'fsdp')
- input_grad: bfloat16 [16, 5120, 5120], P('group', 'fsdp')
- weight_grad: bfloat16 [16, 5120, 1024], P('group', 'fsdp')
- gain_grad: float32 [16, 5120], P('group', 'fsdp')
- new_outer: float32 [5120, 256], P('fsdp')
- new_momentum: float32 [5120, 256], P('fsdp')
The draws below stay inside these ranges and needn't reach their ends.
Inputs may be any that keep to these rules, and one draw needn't show every extreme that they name: `seg_ids`: each of the 16 sequences of a group holds one or more tokens.
All inputs are finite; a program needn't handle non-finite values.
Results may differ from the reference program's by a relative error of at most 0.019.
Values may be sent and summed in bfloat16 or wider, within the bound.
A program may use at most 128 MiB of HBM per device.

```python
import math
import jax
import jax.numpy as jnp
import numpy as np
from jax import lax

D = 5120
TOK_DEV = 320
SEQS = 16
NFRAG = 4
KV = 1024
FC = 256
TOK_GROUP = 5120
N_GROUP = 16
N_FSDP = 16


def block_levels(rng, shape, pieces, smallest, top_value):
    loudness, own = 1.0, jax.random.fold_in(rng, 6)
    for dim, blocks in pieces:
        draws = jnp.exp(jax.random.uniform(jax.random.fold_in(own, dim), (blocks,), jnp.float32, smallest / len(pieces), top_value / len(pieces)))
        loudness = loudness * jnp.repeat(draws, shape[dim] // blocks).reshape([-1 if axis == dim else 1 for axis in range(len(shape))])
    return loudness


def split_up(number_of, total, most, lean):
    loads = [(1 << 20) // math.isqrt(standing ** lean) + 1 for standing in range(2, number_of + 1)]
    rest, counts = total - most - (number_of - 1), [1] * (number_of - 1)
    while rest > 0:
        free = [i for i in range(number_of - 1) if counts[i] < most]
        pool, budget = sum([loads[i] for i in free]), rest
        for i in free:
            addition = min(most - counts[i], max(1, budget * loads[i] // pool), rest)
            counts[i] = counts[i] + addition
            rest = rest - addition
    return np.array([most] + counts)


def uneven(key, amount, total, most, slope):
    if amount == 2:
        one = jax.random.randint(key, (), max(1, total - most), min(most, total - 1) + 1)
        return jnp.stack([one, total - one])
    tallies = jnp.asarray(split_up(amount, total, most, slope), jnp.int32)
    couples = (amount - 1) // 2
    source_of, taker = tallies[1:1 + 2 * couples:2], tallies[2:2 + 2 * couples:2]
    slack = jnp.minimum(source_of - 1, most - taker)
    shifted = jax.random.randint(jax.random.fold_in(key, 1), (couples,), 0, 1 << 20) % (slack + 1)
    tallies = tallies.at[1:1 + 2 * couples:2].set(source_of - shifted).at[2:2 + 2 * couples:2].set(taker + shifted)
    return tallies[jax.random.permutation(jax.random.fold_in(key, 2), amount)]


def scatter_about(key, dims, width, limit, pieces=(), kind=jnp.bfloat16):
    drawn = jax.random.normal(key, dims, jnp.float32) * width
    if len(pieces) > 0:
        drawn = block_levels(key, dims, pieces, -0.22, 0.18) * drawn
    return jnp.clip(drawn, min=-limit, max=limit).astype(kind)


def setup_inputs(seed: int = 0) -> dict:
    key_list = jax.random.split(jax.random.key(seed), 10)
    inputs = scatter_about(key_list[0], (N_GROUP, TOK_GROUP, D), 1.0, 6.0, ((0, 16), (1, 16)))
    key_grad = scatter_about(key_list[1], (N_GROUP, TOK_GROUP, KV), 1.0, 6.0, ((0, 16), (1, 16)))
    seg_ids = jax.vmap(lambda own: jnp.searchsorted(jnp.cumsum(uneven(own, SEQS, TOK_GROUP, TOK_DEV * N_FSDP // 2, 1)), jnp.arange(TOK_GROUP), side="right"))(jax.random.split(key_list[2], N_GROUP)).reshape((N_GROUP, TOK_GROUP)).astype(jnp.int32)
    advantages = scatter_about(key_list[3], (N_GROUP, SEQS), 1.0, 4.0, ((0, 16),), jnp.float32)
    gains = jnp.clip(1.0 + 0.1 * jax.random.normal(key_list[4], (N_GROUP, D), jnp.float32), 0.5, 1.5).astype(jnp.bfloat16)
    local_weights = scatter_about(key_list[5], (N_GROUP, D, KV), 1.0, 6.0, ((0, 16), (1, 16)))
    outer_weights = scatter_about(key_list[6], (D, KV), 1.0, 6.0, ((0, 16),), jnp.float32)
    momentum = scatter_about(key_list[7], (D, KV), 0.5, 3.0, ((0, 16),), jnp.float32)
    frag_index = jax.random.randint(key_list[8], (1,), 0, NFRAG).astype(jnp.int32)
    return {"inputs": inputs, "key_grad": key_grad, "seg_ids": seg_ids, "advantages": advantages, "gains": gains, "local_weights": local_weights, "outer_weights": outer_weights, "momentum": momentum, "frag_index": frag_index}


EPSILON = 1e-06
OUTER_MU = 0.9
OUTER_LR = 0.7

def group_pass(operands):
    inputs, key_grad, seg_ids, advantages, gains, weights = operands
    unit_scale = D ** (-0.5)
    float_in = inputs.astype(jnp.float32)
    inv_rms = lax.rsqrt(lax.optimization_barrier(jnp.mean(float_in * float_in, -1, keepdims=True)) + EPSILON)
    unit_rows = float_in * inv_rms
    gain_float = gains.astype(jnp.float32)
    normed = (unit_rows * gain_float).astype(jnp.bfloat16)
    keys = (jnp.dot(normed, weights, preferred_element_type=jnp.float32) * unit_scale).astype(jnp.bfloat16)
    onehot = seg_ids[:, None] == jnp.arange(SEQS, dtype=jnp.int32)[None, :]
    lengths = lax.optimization_barrier(jnp.sum(onehot.astype(jnp.int32), 0))
    floor_len = TOK_DEV * N_FSDP / (2 * SEQS)
    per_seq = advantages * (TOK_DEV * N_FSDP / SEQS) / jnp.maximum(lengths.astype(jnp.float32), floor_len)
    token_weight = lax.optimization_barrier(jnp.sum(jnp.where(onehot, per_seq[None, :], jnp.float32(0.0)), 1))
    cotangent = (key_grad.astype(jnp.float32) * token_weight[:, None]).astype(jnp.bfloat16)
    grad_norm = lax.dot_general(cotangent, weights, (((1,), (1,)), ((), ())), preferred_element_type=jnp.float32) * unit_scale
    scaled_grad = grad_norm * gain_float
    input_grad = (inv_rms * (scaled_grad - unit_rows * lax.optimization_barrier(jnp.mean(scaled_grad * unit_rows, -1, keepdims=True)))).astype(jnp.bfloat16)
    normed_blocks = normed.reshape(N_FSDP, TOK_DEV, D)
    cot_blocks = cotangent.reshape(N_FSDP, TOK_DEV, KV)
    grad_blocks = grad_norm.reshape(N_FSDP, TOK_DEV, D)
    unit_blocks = unit_rows.reshape(N_FSDP, TOK_DEV, D)

    def block_terms(carry, block):
        normed_block, cot_block, grad_block, unit_block = block
        weight_term = (jnp.dot(normed_block.T, cot_block, preferred_element_type=jnp.float32) * unit_scale).astype(jnp.bfloat16)
        gain_term = lax.optimization_barrier(jnp.sum(grad_block * unit_block, 0)).astype(jnp.bfloat16)
        return ((carry[0] + weight_term.astype(jnp.float32), carry[1] + gain_term.astype(jnp.float32)), None)
    start_sums = (jnp.zeros((D, KV), jnp.float32), jnp.zeros((D,), jnp.float32))
    sums, unused = lax.scan(block_terms, start_sums, (normed_blocks, cot_blocks, grad_blocks, unit_blocks))
    return (keys, input_grad, sums[0].astype(jnp.bfloat16), sums[1])

def reference(inputs, key_grad, seg_ids, advantages, gains, local_weights, outer_weights, momentum, frag_index):
    keys, input_grad, weight_grad, gain_grad = lax.map(group_pass, (inputs, key_grad, seg_ids, advantages, gains, local_weights))
    fragment = frag_index[0].astype(jnp.int32) * FC
    outer_frag = lax.dynamic_slice_in_dim(outer_weights, fragment, FC, 1)
    moment_frag = lax.dynamic_slice_in_dim(momentum, fragment, FC, 1)
    local_frag = lax.dynamic_slice_in_dim(local_weights, fragment, FC, 2).astype(jnp.float32)
    pseudo_grad = lax.optimization_barrier(jnp.sum(outer_frag[None] - local_frag, 0)) / N_GROUP
    new_momentum = OUTER_MU * moment_frag + pseudo_grad
    new_outer = outer_frag - OUTER_LR * (pseudo_grad + OUTER_MU * new_momentum)
    return (keys, input_grad, weight_grad, gain_grad, new_outer, new_momentum)
```

```python
import functools

import jax
import jax.numpy as jnp
from jax import lax
from jax.experimental import pallas as pl
from jax.experimental.pallas import tpu as pltpu
from jax.sharding import PartitionSpec as P

MESH = pl.DeviceIdType.MESH
F32 = jnp.float32
BF16 = jnp.bfloat16
EPSILON = 1e-06
OUTER_MU = 0.9
OUTER_LR = 0.7
NFRAG = 4
RING = 8
PAIRS = 4
STEPS = 7

GATHER = (
    ((0, 0), (0, 1), (1, 0), (1, 1), (2, 0), (2, 1), (3, 0)),
    ((0, 1), (0, 0), (1, 1), (1, 0), (2, 1), (2, 0), (3, 1)),
)
SCATTER = (
    ((4, 0), (3, 1), (3, 0), (2, 1), (2, 0), (1, 1), (1, 0)),
    ((4, 1), (3, 0), (3, 1), (2, 0), (2, 1), (1, 0), (1, 1)),
)


def to_column(row, n):
    here = lax.broadcasted_iota(jnp.int32, (n, n), 0) == lax.broadcasted_iota(jnp.int32, (n, n), 1)
    return jnp.sum(jnp.where(here, jnp.broadcast_to(row, (n, n)), 0.0), axis=1, keepdims=True)


def to_row(column, n):
    here = lax.broadcasted_iota(jnp.int32, (n, n), 0) == lax.broadcasted_iota(jnp.int32, (n, n), 1)
    return jnp.sum(jnp.where(here, jnp.broadcast_to(column, (n, n)), 0.0), axis=0, keepdims=True)


def kernel(
    inputs, key_grad, seg, adv, gains, weights, outer, moment, frag,
    keys_out, ig_out, wg_out, gg_out, no_out, nm_out,
    x_mine, x_other, w_all, cots, kg, lw, ow, mom, inv, gain_col, weighted,
    u_all, rs_send, rs_recv, sg_mine, sg_send, sg_recv, k_mine, k_send, k_recv,
    ig_buf, k_buf, wg_buf, cnt_own, cnt_recv,
    pg_own, pg_a, pg_s1, pg_b, pg_s2, pg_c, pg_full, pg_e,
    load_sem, store_sem, ag_ss, ag_rs, rs_ss, rs_rs, x_ss, x_rs, cnt_ss, cnt_rs, pg_ss, pg_rs,
):
    tok, width = inputs.shape
    kv = key_grad.shape[1]
    rows = weights.shape[0]
    half = rows // 2
    pair = 2 * rows
    mid = width // 2
    cols = kv // NFRAG
    seqs = adv.shape[1]

    g, f = lax.axis_index("group"), lax.axis_index("fsdp")
    xhi, z = f // RING, lax.rem(f, RING)
    core, y = lax.rem(g, 2), g // 4
    par = lax.rem(z, 2)
    up = xhi * RING + lax.rem(z + 1, RING)
    down = xhi * RING + lax.rem(z + RING - 1, RING)
    across = (1 - xhi) * RING + z
    other_core = g + 1 - 2 * core
    xlo = lax.rem(g // 2, 2)
    side = g + 2 - 4 * xlo
    j = z // 2
    place = (j, lax.rem(j + 3 + 2 * par, 4), lax.rem(j + 1 + 2 * par, 4), lax.rem(j + 2, 4))

    barrier = pltpu.get_barrier_semaphore()
    for i in range(1, 2 * RING):
        pl.semaphore_signal(
            barrier, inc=1, device_id={"fsdp": lax.rem(f + i, 2 * RING)}, device_id_type=MESH
        )
    group_peers = [other_core, side] + [lax.rem(g + 4 * i, 16) for i in (1, 2, 3)]
    for p in group_peers:
        pl.semaphore_signal(barrier, inc=1, device_id={"group": p}, device_id_type=MESH)

    def load(src, dst, i):
        c = pltpu.make_async_copy(src, dst, load_sem.at[i])
        c.start()
        return c

    def col(start):
        return pl.ds(pl.multiple_of(start, 128), pair)

    lw_load = load(weights, lw, 0)
    x_loads = []
    for p in range(PAIRS):
        x_loads.append(load(inputs.at[:, col(xhi * mid + place[p] * pair)], x_mine.at[p, pl.ds(0, tok)], 1 + p))
        x_loads.append(load(inputs.at[:, col((1 - xhi) * mid + place[p] * pair)], x_other.at[p], 5 + p))
    kg_load = load(key_grad, kg, 9)
    ow_load = load(outer, ow, 10)
    mom_load = load(moment, mom, 11)

    seg_col = to_column(seg[...].astype(F32), tok)
    lane = lax.broadcasted_iota(jnp.int32, (tok, 128), 1).astype(F32)
    onehot = jnp.where(jnp.broadcast_to(seg_col, (tok, 128)) == lane, 1.0, 0.0)
    counts = jnp.sum(onehot, axis=0, keepdims=True)
    cnt_own[...] = jnp.broadcast_to(counts, (8, 128))

    gain_col[...] = to_column(gains[...].astype(F32), rows)
    lw_load.wait()
    base = z * rows

    def scale_rows(t, c):
        r = pl.ds(pl.multiple_of(t * 32, 32), 32)
        w_all[pl.ds(pl.multiple_of(base + t * 32, 32), 32)] = (
            lw[r].astype(F32) * gain_col[r]
        ).astype(BF16)
        return c

    lax.fori_loop(0, rows // 32, scale_rows, 0)
    pl.semaphore_wait(barrier, 2 * RING - 1 + len(group_peers))

    def ring_to(way):
        return {"fsdp": up if way == 0 else down}

    def block_rows(way, distance, h, outward):
        sign = 1 if (way == 0) == outward else -1
        b = lax.rem(z + sign * distance + RING, RING)
        return pl.ds(pl.multiple_of(b * rows + h * half, 16), half)

    def gather(way, k):
        distance, h = GATHER[way][k]
        r = block_rows(way, distance, h, False)
        return pltpu.make_async_remote_copy(
            src_ref=w_all.at[r], dst_ref=w_all.at[r], send_sem=ag_ss.at[way, k],
            recv_sem=ag_rs.at[way, k], device_id=ring_to(way), device_id_type=MESH,
        )

    ag = [[gather(way, k) for k in range(STEPS)] for way in (0, 1)]

    def gather_start(k):
        for way in (0, 1):
            ag[way][k].start()

    def gather_step(k):
        for way in (0, 1):
            ag[way][k].wait_recv()
            if k + 2 < STEPS:
                ag[way][k + 2].start()

    gather_start(0)

    cnt = []
    for i in range(1, 2 * RING):
        cnt.append(pltpu.make_async_remote_copy(
            src_ref=cnt_own, dst_ref=cnt_recv.at[i], send_sem=cnt_ss.at[i], recv_sem=cnt_rs.at[i],
            device_id={"fsdp": lax.rem(f + i, 2 * RING)}, device_id_type=MESH,
        ))
        cnt[-1].start()

    def cross(src, dst, i):
        return pltpu.make_async_remote_copy(
            src_ref=src, dst_ref=dst, send_sem=x_ss.at[i], recv_sem=x_rs.at[i],
            device_id={"fsdp": across}, device_id_type=MESH,
        )

    x_cross = [
        cross(inputs.at[:, col((1 - xhi) * mid + place[p] * pair)], x_mine.at[p, pl.ds(tok, tok)], p)
        for p in range(PAIRS)
    ]
    cots_cross = cross(cots.at[pl.ds(0, tok)], cots.at[pl.ds(tok, tok)], 4)
    sg_cross = [cross(sg_send.at[p], sg_recv.at[p], 5 + p) for p in range(PAIRS)]
    k_cross = cross(k_send, k_recv, 9)

    x_cross[3].start()
    gather_start(1)

    chosen = frag[0]

    def pick(ref, r):
        out = ref[r, pl.ds(0, cols)].astype(F32)
        for i in range(1, NFRAG):
            out = jnp.where(chosen == i, ref[r, pl.ds(i * cols, cols)].astype(F32), out)
        return out

    def pick_local(t, c):
        r = pl.ds(pl.multiple_of(t * 32, 32), 32)
        pg_own[r] = pick(lw, r).astype(BF16)
        return c

    lax.fori_loop(0, rows // 32, pick_local, 0)

    def to_group(src, dst, i, peer):
        return pltpu.make_async_remote_copy(
            src_ref=src, dst_ref=dst, send_sem=pg_ss.at[i], recv_sem=pg_rs.at[i],
            device_id={"group": peer}, device_id_type=MESH,
        )

    mine_r = pl.ds(pl.multiple_of(core * half, 16), half)
    theirs_r = pl.ds(pl.multiple_of((1 - core) * half, 16), half)
    quarter = half // 4
    pg_first = to_group(pg_own.at[theirs_r], pg_a, 0, other_core)
    pg_first.start()

    for c in x_loads:
        c.wait()

    def mean_square(t, c):
        r = pl.ds(pl.multiple_of(t * 16, 16), 16)
        total = jnp.zeros((16, pair), F32)
        for p in range(PAIRS):
            a, b = x_mine[p, r].astype(F32), x_other[p, r].astype(F32)
            total = total + a * a + b * b
        inv[r] = lax.rsqrt(jnp.sum(total, axis=1, keepdims=True) * (1.0 / width) + EPSILON)
        return c

    lax.fori_loop(0, tok // 16, mean_square, 0)

    lengths = counts
    for i, c in enumerate(cnt):
        c.wait_recv()
        lengths = lengths + cnt_recv[i + 1, pl.ds(0, 1), :]
    group_tokens = tok * 2 * RING
    per_seq = (
        adv[...] * (group_tokens / seqs)
        / jnp.maximum(lengths[:, :seqs], group_tokens / (2 * seqs))
    )
    token_weight = jnp.sum(onehot[:, :seqs] * per_seq, axis=1, keepdims=True)
    weighted[...] = token_weight * inv[...] * (width ** -0.5)
    kg_load.wait()

    def scale_tokens(t, c):
        r = pl.ds(pl.multiple_of(t * 32, 32), 32)
        cots[r] = (kg[r].astype(F32) * weighted[r]).astype(BF16)
        return c

    lax.fori_loop(0, tok // 32, scale_tokens, 0)
    cots_cross.start()
    x_cross[2].start()

    n_tile = 256

    def u_pair(p):
        across_t = x_mine[p].T

        def body(n, c):
            at = pl.ds(pl.multiple_of(n * n_tile, n_tile), n_tile)
            u_all[pl.ds(pl.multiple_of(place[p] * pair, 16), pair), at] = jnp.dot(
                across_t, cots[:, at], preferred_element_type=F32
            )
            return c

        lax.fori_loop(0, kv // n_tile, body, 0)

    def sg_part(p, r):
        w = w_all[pl.ds(pl.multiple_of(place[p] * pair, 16), pair)]
        return lax.dot_general(
            cots[r], w, (((1,), (1,)), ((), ())), preferred_element_type=F32
        )

    def sg_theirs(p):
        sg_send[p] = sg_part(p, pl.ds(tok, tok)).astype(BF16)
        sg_cross[p].start()

    def sg_ours(p):
        sg_mine[p] = sg_part(p, pl.ds(0, tok))

    def keys_half(first, out, kind):
        def body(n, c):
            at = pl.ds(pl.multiple_of(n * n_tile, n_tile), n_tile)
            total = jnp.zeros((tok, n_tile), F32)
            for p in range(PAIRS):
                total = total + jnp.dot(
                    x_mine[p, pl.ds(first, tok)],
                    w_all[pl.ds(pl.multiple_of(place[p] * pair, 16), pair), at],
                    preferred_element_type=F32,
                )
            out[:, at] = total.astype(kind)
            return c

        lax.fori_loop(0, kv // n_tile, body, 0)

    def scatter(way, k):
        return pltpu.make_async_remote_copy(
            src_ref=rs_send.at[way, k], dst_ref=rs_recv.at[way, k], send_sem=rs_ss.at[way, k],
            recv_sem=rs_rs.at[way, k], device_id=ring_to(way), device_id_type=MESH,
        )

    rs = [[scatter(way, k) for k in range(STEPS)] for way in (0, 1)]

    def scatter_send(k):
        for way in (0, 1):
            distance, h = SCATTER[way][k]
            b = block_rows(way, distance, h, True)
            if k >= 2:
                rs[way][k - 2].wait_recv()

            def body(t, c, way=way, b=b, k=k):
                r = pl.ds(pl.multiple_of(t * 32, 32), 32)
                term = u_all[pl.ds(pl.multiple_of(b.start + t * 32, 32), 32)]
                if k >= 2:
                    term = term + rs_recv[way, k - 2, r].astype(F32)
                rs_send[way, k, r] = term.astype(BF16)
                return c

            lax.fori_loop(0, half // 32, body, 0)
            rs[way][k].start()

    gather_step(0)
    pg_first.wait_recv()
    pg_s1[...] = pg_own[mine_r].astype(F32) + pg_a[...].astype(F32)
    pg_second = []
    for i in (1, 2, 3):
        yy = lax.rem(y + i, 4)
        pg_second.append(to_group(
            pg_s1.at[pl.ds(pl.multiple_of(yy * quarter, 8), quarter)], pg_b.at[i], i, lax.rem(g + 4 * i, 16)
        ))
        pg_second[-1].start()
    gather_step(1)
    x_cross[1].start()
    for c in pg_second:
        c.wait_recv()
    own_q = pl.ds(pl.multiple_of(y * quarter, 8), quarter)
    pg_s2[...] = pg_s1[own_q] + pg_b[1] + pg_b[2] + pg_b[3]
    pg_third = to_group(pg_s2, pg_c, 4, side)
    pg_third.start()
    gather_step(2)
    x_cross[0].start()
    pg_third.wait_recv()
    pg_full[own_q] = pg_s2[...] + pg_c[...]
    pg_fourth = []
    for i in (1, 2, 3):
        pg_fourth.append(to_group(pg_full.at[own_q], pg_full.at[own_q], 4 + i, lax.rem(g + 4 * i, 16)))
        pg_fourth[-1].start()
    cots_cross.wait_recv()
    x_cross[3].wait_recv()
    u_pair(3)
    gather_step(3)
    sg_theirs(0)
    for c in pg_fourth:
        c.wait_recv()
    pg_fifth = to_group(pg_full, pg_e, 8, other_core)
    pg_fifth.start()
    x_cross[2].wait_recv()
    u_pair(2)
    gather_step(4)
    scatter_send(0)
    scatter_send(1)
    sg_theirs(1)
    x_cross[1].wait_recv()
    u_pair(1)
    gather_step(5)
    sg_theirs(2)
    gather_step(6)
    sg_theirs(3)
    scatter_send(2)
    x_cross[0].wait_recv()
    u_pair(0)
    scatter_send(3)
    keys_half(tok, k_send, BF16)
    k_cross.start()
    sg_ours(0)
    scatter_send(4)
    sg_ours(1)
    sg_ours(2)
    scatter_send(5)
    sg_ours(3)

    pg_fifth.wait_recv()
    ow_load.wait()
    mom_load.wait()

    def outer_half(r, total_ref):
        def body(t, c):
            rr = pl.ds(pl.multiple_of(r.start + t * 32, 32), 32)
            o, m = pick(ow, rr), pick(mom, rr)
            pseudo = o - total_ref[pl.ds(pl.multiple_of(t * 32, 32), 32)] * (1.0 / 16)
            new_m = OUTER_MU * m + pseudo
            nm_out[rr] = new_m
            no_out[rr] = o - OUTER_LR * (pseudo + OUTER_MU * new_m)
            return c

        lax.fori_loop(0, half // 32, body, 0)

    outer_half(mine_r, pg_full)
    outer_half(theirs_r, pg_e)
    scatter_send(6)
    keys_half(0, k_mine, F32)

    for p in (0, 1, 2, 3):
        sg_cross[p].wait_recv()

    def finish_rows(t, c):
        r = pl.ds(pl.multiple_of(t * 16, 16), 16)
        total = jnp.zeros((16, pair), F32)
        for p in range(PAIRS):
            total = total + sg_mine[p, r] * x_mine[p, r].astype(F32)
            total = total + sg_recv[p, r].astype(F32) * x_other[p, r].astype(F32)
        i = inv[r]
        m = jnp.sum(total, axis=1, keepdims=True) * (1.0 / width) * i * i
        for p in range(PAIRS):
            ig_buf[p, r] = (sg_mine[p, r] - m * x_mine[p, r].astype(F32)).astype(BF16)
            ig_buf[PAIRS + p, r] = (
                sg_recv[p, r].astype(F32) - m * x_other[p, r].astype(F32)
            ).astype(BF16)
        return c

    lax.fori_loop(0, tok // 16, finish_rows, 0)
    stores = []

    def store(src, dst, i):
        c = pltpu.make_async_copy(src, dst, store_sem.at[i])
        c.start()
        stores.append(c)

    for p in range(PAIRS):
        store(ig_buf.at[p], ig_out.at[:, col(xhi * mid + place[p] * pair)], p)
        store(ig_buf.at[PAIRS + p], ig_out.at[:, col((1 - xhi) * mid + place[p] * pair)], PAIRS + p)

    k_cross.wait_recv()

    def finish_keys(t, c):
        r = pl.ds(pl.multiple_of(t * 32, 32), 32)
        k_buf[r] = ((k_mine[r] + k_recv[r].astype(F32)) * (inv[r] * (width ** -0.5))).astype(BF16)
        return c

    lax.fori_loop(0, tok // 32, finish_keys, 0)
    store(k_buf, keys_out, 8)

    for k in (5, 6):
        for way in (0, 1):
            rs[way][k].wait_recv()
    gain_sum = []
    for h in (0, 1):
        k_up, k_down = (6, 5) if h == 0 else (5, 6)

        def body(t, c, h=h, k_up=k_up, k_down=k_down):
            r = pl.ds(pl.multiple_of(t * 32, 32), 32)
            rr = pl.ds(pl.multiple_of(h * half + t * 32, 32), 32)
            total = u_all[pl.ds(pl.multiple_of(base + h * half + t * 32, 32), 32)]
            total = total + rs_recv[0, k_up, r].astype(F32) + rs_recv[1, k_down, r].astype(F32)
            wg_buf[rr] = (total * gain_col[rr]).astype(BF16)
            weighted[rr] = jnp.sum(total * lw[rr].astype(F32), axis=1, keepdims=True)
            return c

        lax.fori_loop(0, half // 32, body, 0)
    store(wg_buf, wg_out, 9)
    gg_out[...] = to_row(weighted[...], rows)

    for c in stores:
        c.wait()
    for way in (0, 1):
        for k in range(STEPS):
            ag[way][k].wait_send()
            rs[way][k].wait_send()
    for c in cnt + x_cross + sg_cross + [cots_cross, k_cross, pg_first, pg_third, pg_fifth]:
        c.wait_send()
    for c in pg_second + pg_fourth:
        c.wait_send()


def local(
    inputs, key_grad, seg_ids, advantages, gains, local_weights, outer_weights, momentum, frag_index
):
    tok, width = inputs.shape[1:]
    kv, rows = key_grad.shape[2], local_weights.shape[1]
    half, pair, cols = rows // 2, 2 * rows, kv // NFRAG
    hbm, vmem = pl.BlockSpec(memory_space=pl.ANY), pl.BlockSpec(memory_space=pltpu.VMEM)
    dma = pltpu.SemaphoreType.DMA
    scratch = [
        pltpu.VMEM((PAIRS, 2 * tok, pair), BF16),
        pltpu.VMEM((PAIRS, tok, pair), BF16),
        pltpu.VMEM((RING * rows, kv), BF16),
        pltpu.VMEM((2 * tok, kv), BF16),
        pltpu.VMEM((tok, kv), BF16),
        pltpu.VMEM((rows, kv), BF16),
        pltpu.VMEM((rows, kv), F32),
        pltpu.VMEM((rows, kv), F32),
        pltpu.VMEM((tok, 1), F32),
        pltpu.VMEM((rows, 1), F32),
        pltpu.VMEM((tok, 1), F32),
        pltpu.VMEM((RING * rows, kv), F32),
        pltpu.VMEM((2, STEPS, half, kv), BF16),
        pltpu.VMEM((2, STEPS, half, kv), BF16),
        pltpu.VMEM((PAIRS, tok, pair), F32),
        pltpu.VMEM((PAIRS, tok, pair), BF16),
        pltpu.VMEM((PAIRS, tok, pair), BF16),
        pltpu.VMEM((tok, kv), F32),
        pltpu.VMEM((tok, kv), BF16),
        pltpu.VMEM((tok, kv), BF16),
        pltpu.VMEM((2 * PAIRS, tok, pair), BF16),
        pltpu.VMEM((tok, kv), BF16),
        pltpu.VMEM((rows, kv), BF16),
        pltpu.VMEM((8, 128), F32),
        pltpu.VMEM((2 * RING, 8, 128), F32),
        pltpu.VMEM((rows, cols), BF16),
        pltpu.VMEM((half, cols), BF16),
        pltpu.VMEM((half, cols), F32),
        pltpu.VMEM((4, half // 4, cols), F32),
        pltpu.VMEM((half // 4, cols), F32),
        pltpu.VMEM((half // 4, cols), F32),
        pltpu.VMEM((half, cols), F32),
        pltpu.VMEM((half, cols), F32),
        dma((12,)), dma((10,)),
        dma((2, STEPS)), dma((2, STEPS)), dma((2, STEPS)), dma((2, STEPS)),
        dma((10,)), dma((10,)), dma((2 * RING,)), dma((2 * RING,)), dma((9,)), dma((9,)),
    ]
    flops = 6 * 2 * tok * (width // 2) * kv
    out = pl.pallas_call(
        kernel,
        out_shape=[
            jax.ShapeDtypeStruct((tok, kv), BF16),
            jax.ShapeDtypeStruct((tok, width), BF16),
            jax.ShapeDtypeStruct((rows, kv), BF16),
            jax.ShapeDtypeStruct((1, rows), F32),
            jax.ShapeDtypeStruct((rows, cols), F32),
            jax.ShapeDtypeStruct((rows, cols), F32),
        ],
        in_specs=[
            hbm, hbm, vmem, vmem, vmem, hbm, hbm, hbm, pl.BlockSpec(memory_space=pltpu.SMEM),
        ],
        out_specs=[hbm, hbm, hbm, vmem, vmem, vmem],
        scratch_shapes=scratch,
        compiler_params=pltpu.CompilerParams(
            collective_id=0, has_side_effects=True, vmem_limit_bytes=62 * 2**20
        ),
        cost_estimate=pl.CostEstimate(flops=flops, bytes_accessed=20 * 2**20, transcendentals=0),
        name="key_projection",
    )(
        inputs[0], key_grad[0], seg_ids, advantages, gains, local_weights[0],
        outer_weights, momentum, frag_index,
    )
    keys, input_grad, weight_grad, gain_grad, new_outer, new_momentum = out
    return keys[None], input_grad[None], weight_grad[None], gain_grad, new_outer, new_momentum


def solution(mesh):
    in_specs = (
        P("group", "fsdp", None),
        P("group", "fsdp", None),
        P("group", "fsdp"),
        P("group", None),
        P("group", "fsdp"),
        P("group", "fsdp", None),
        P("fsdp", None),
        P("fsdp", None),
        P(),
    )
    out_specs = (
        P("group", "fsdp", None),
        P("group", "fsdp", None),
        P("group", "fsdp", None),
        P("group", "fsdp"),
        P("fsdp", None),
        P("fsdp", None),
    )
    return jax.shard_map(local, mesh=mesh, in_specs=in_specs, out_specs=out_specs, check_vma=False)
```

```python
import functools

import jax
import jax.numpy as jnp
from jax import lax
from jax.experimental import pallas as pl
from jax.experimental.pallas import tpu as pltpu
from jax.sharding import PartitionSpec as P

MESH = pl.DeviceIdType.MESH
F32 = jnp.float32
BF16 = jnp.bfloat16
EPSILON = 1e-06
OUTER_MU = 0.9
OUTER_LR = 0.7
NFRAG = 4
RING = 8
PAIRS = 4
STEPS = 7

GATHER = (
    ((0, 0), (0, 1), (1, 0), (1, 1), (2, 0), (2, 1), (3, 0)),
    ((0, 1), (0, 0), (1, 1), (1, 0), (2, 1), (2, 0), (3, 1)),
)
SCATTER = (
    ((4, 0), (3, 1), (3, 0), (2, 1), (2, 0), (1, 1), (1, 0)),
    ((4, 1), (3, 0), (3, 1), (2, 0), (2, 1), (1, 0), (1, 1)),
)


def to_column(row, n):
    here = lax.broadcasted_iota(jnp.int32, (n, n), 0) == lax.broadcasted_iota(jnp.int32, (n, n), 1)
    return jnp.sum(jnp.where(here, jnp.broadcast_to(row, (n, n)), 0.0), axis=1, keepdims=True)


def to_row(column, n):
    here = lax.broadcasted_iota(jnp.int32, (n, n), 0) == lax.broadcasted_iota(jnp.int32, (n, n), 1)
    return jnp.sum(jnp.where(here, jnp.broadcast_to(column, (n, n)), 0.0), axis=0, keepdims=True)


def kernel(
    inputs, key_grad, seg, adv, gains, weights, frag,
    k_buf, ig_buf, wg_buf, gg_out, pg_total,
    x_mine, x_other, w_all, cots, kg, lw, inv, gain_col, weighted,
    u_all, rs_send, rs_recv, sg_mine, sg_send, sg_recv, k_mine, k_send, k_recv,
    cnt_own, cnt_recv, pg_own, pg_a, pg_s1, pg_b, pg_s2, pg_c,
    load_sem, ag_ss, ag_rs, rs_ss, rs_rs, x_ss, x_rs, cnt_ss, cnt_rs, pg_ss, pg_rs,
):
    tok, width = inputs.shape
    kv = key_grad.shape[1]
    rows = weights.shape[0]
    half = rows // 2
    pair = 2 * rows
    mid = width // 2
    cols = kv // NFRAG
    quarter = rows // 4
    seqs = adv.shape[1]

    g, f = lax.axis_index("group"), lax.axis_index("fsdp")
    xhi, z = f // RING, lax.rem(f, RING)
    par = lax.rem(z, 2)
    up = xhi * RING + lax.rem(z + 1, RING)
    down = xhi * RING + lax.rem(z + RING - 1, RING)
    across = (1 - xhi) * RING + z
    core, y = lax.rem(g, 2), g // 4
    side = g + 2 - 4 * lax.rem(g // 2, 2)
    other_core = g + 1 - 2 * core
    over_y = [lax.rem(g + 4 * i, 16) for i in (1, 2, 3)]
    j = z // 2
    place = (j, lax.rem(j + 3 + 2 * par, 4), lax.rem(j + 1 + 2 * par, 4), lax.rem(j + 2, 4))

    barrier = pltpu.get_barrier_semaphore()
    ring = [xhi * RING + lax.rem(z + i, RING) for i in range(1, RING)]
    for peer in ring + [across]:
        pl.semaphore_signal(barrier, inc=1, device_id={"fsdp": peer}, device_id_type=MESH)
    for peer in over_y + [side]:
        pl.semaphore_signal(barrier, inc=1, device_id={"group": peer}, device_id_type=MESH)

    @pl.when(core == 0)
    def _():
        pl.semaphore_signal(barrier, inc=1, device_id={"group": other_core}, device_id_type=MESH)

    def load(src, dst, i):
        c = pltpu.make_async_copy(src, dst, load_sem.at[i])
        c.start()
        return c

    def col(start):
        return pl.ds(pl.multiple_of(start, 128), pair)

    lw_load = load(weights, lw, 0)
    x_loads = []
    for p in range(PAIRS):
        x_loads.append(load(inputs.at[:, col(xhi * mid + place[p] * pair)], x_mine.at[p, pl.ds(0, tok)], 1 + p))
        x_loads.append(load(inputs.at[:, col((1 - xhi) * mid + place[p] * pair)], x_other.at[p], 5 + p))
    kg_load = load(key_grad, kg, 9)

    gain_col[...] = to_column(gains[...].astype(F32), rows)
    lw_load.wait()
    base = z * rows

    def scale_rows(t, c):
        r = pl.ds(pl.multiple_of(t * 32, 32), 32)
        w_all[pl.ds(pl.multiple_of(base + t * 32, 32), 32)] = (
            lw[r].astype(F32) * gain_col[r]
        ).astype(BF16)
        return c

    lax.fori_loop(0, rows // 32, scale_rows, 0)
    pl.semaphore_wait(barrier, RING + 4 + core)

    def ring_to(way):
        return {"fsdp": up if way == 0 else down}

    def block_rows(way, distance, h, outward):
        sign = 1 if (way == 0) == outward else -1
        b = lax.rem(z + sign * distance + RING, RING)
        return pl.ds(pl.multiple_of(b * rows + h * half, 16), half)

    def gather(way, k):
        distance, h = GATHER[way][k]
        r = block_rows(way, distance, h, False)
        return pltpu.make_async_remote_copy(
            src_ref=w_all.at[r], dst_ref=w_all.at[r], send_sem=ag_ss.at[way, k],
            recv_sem=ag_rs.at[way, k], device_id=ring_to(way), device_id_type=MESH,
        )

    ag = [[gather(way, k) for k in range(STEPS)] for way in (0, 1)]

    def gather_start(k):
        for way in (0, 1):
            ag[way][k].start()

    def gather_step(k):
        for way in (0, 1):
            ag[way][k].wait_recv()
            if k + 2 < STEPS:
                ag[way][k + 2].start()

    def cross(src, dst, i):
        return pltpu.make_async_remote_copy(
            src_ref=src, dst_ref=dst, send_sem=x_ss.at[i], recv_sem=x_rs.at[i],
            device_id={"fsdp": across}, device_id_type=MESH,
        )

    x_cross = [
        cross(inputs.at[:, col((1 - xhi) * mid + place[p] * pair)], x_mine.at[p, pl.ds(tok, tok)], p)
        for p in range(PAIRS)
    ]
    cots_cross = cross(cots.at[pl.ds(0, tok)], cots.at[pl.ds(tok, tok)], 4)
    sg_cross = [cross(sg_send.at[p], sg_recv.at[p], 5 + p) for p in range(PAIRS)]
    k_cross = cross(k_send, k_recv, 9)

    gather_start(0)
    x_cross[3].start()
    gather_start(1)

    seg_col = to_column(seg[...].astype(F32), tok)
    lane = lax.broadcasted_iota(jnp.int32, (tok, 128), 1).astype(F32)
    onehot = jnp.where(jnp.broadcast_to(seg_col, (tok, 128)) == lane, 1.0, 0.0)
    counts = jnp.sum(onehot, axis=0, keepdims=True)
    cnt_own[0] = jnp.broadcast_to(counts, (8, 128))

    def count_copy(src, dst, i, peer):
        c = pltpu.make_async_remote_copy(
            src_ref=src, dst_ref=dst, send_sem=cnt_ss.at[i], recv_sem=cnt_rs.at[i],
            device_id={"fsdp": peer}, device_id_type=MESH,
        )
        c.start()
        return c

    cnt = [count_copy(cnt_own.at[0], cnt_recv.at[0], 0, across)]
    x_cross[2].start()

    chosen = frag[0]

    def pick_rows(t, c):
        r = pl.ds(pl.multiple_of(t * 32, 32), 32)
        out = lw[r, pl.ds(0, cols)].astype(F32)
        for i in range(1, NFRAG):
            out = jnp.where(chosen == i, lw[r, pl.ds(i * cols, cols)].astype(F32), out)
        pg_own[r] = out.astype(BF16)
        return c

    def to_group(src, dst, i, peer):
        return pltpu.make_async_remote_copy(
            src_ref=src, dst_ref=dst, send_sem=pg_ss.at[i], recv_sem=pg_rs.at[i],
            device_id={"group": peer}, device_id_type=MESH,
        )

    def rows_of(yy):
        return pl.ds(pl.multiple_of(yy * quarter, 16), quarter)

    pg_first = [
        to_group(pg_own.at[rows_of(lax.rem(y + i, 4))], pg_a.at[i], i, over_y[i - 1]) for i in (1, 2, 3)
    ]
    pg_second = to_group(pg_s1, pg_b, 4, side)
    pg_third = to_group(pg_s2, pg_c, 5, other_core)
    pg_last = [
        to_group(pg_total.at[rows_of(y)], pg_total.at[rows_of(y)], 5 + i, over_y[i - 1])
        for i in (1, 2, 3)
    ]

    for c in x_loads:
        c.wait()

    def mean_square(t, c):
        r = pl.ds(pl.multiple_of(t * 16, 16), 16)
        total = jnp.zeros((16, pair), F32)
        for p in range(PAIRS):
            a, b = x_mine[p, r].astype(F32), x_other[p, r].astype(F32)
            total = total + a * a + b * b
        inv[r] = lax.rsqrt(jnp.sum(total, axis=1, keepdims=True) * (1.0 / width) + EPSILON)
        return c

    lax.fori_loop(0, tok // 16, mean_square, 0)
    lax.fori_loop(0, rows // 32, pick_rows, 0)
    for c in pg_first:
        c.start()

    gather_step(0)
    cnt[0].wait_recv()
    cnt_own[1] = cnt_own[0] + cnt_recv[0]
    for i in range(1, RING):
        cnt.append(count_copy(cnt_own.at[1], cnt_recv.at[i], i, ring[i - 1]))
    for c in pg_first:
        c.wait_recv()
    pg_s1[...] = (
        pg_own[rows_of(y)].astype(F32) + pg_a[1].astype(F32) + pg_a[2].astype(F32)
        + pg_a[3].astype(F32)
    )
    pg_second.start()
    gather_step(1)
    lengths = cnt_own[1, pl.ds(0, 1), :]
    for i in range(1, RING):
        cnt[i].wait_recv()
        lengths = lengths + cnt_recv[i, pl.ds(0, 1), :]

    group_tokens = tok * 2 * RING
    per_seq = (
        adv[...] * (group_tokens / seqs)
        / jnp.maximum(lengths[:, :seqs], group_tokens / (2 * seqs))
    )
    token_weight = jnp.sum(onehot[:, :seqs] * per_seq, axis=1, keepdims=True)
    weighted[...] = token_weight * inv[...] * (width ** -0.5)
    kg_load.wait()

    def scale_tokens(t, c):
        r = pl.ds(pl.multiple_of(t * 32, 32), 32)
        cots[r] = (kg[r].astype(F32) * weighted[r]).astype(BF16)
        return c

    lax.fori_loop(0, tok // 32, scale_tokens, 0)
    cots_cross.start()

    n_tile = 256

    def u_pair(p):
        across_t = x_mine[p].T

        def body(n, c):
            at = pl.ds(pl.multiple_of(n * n_tile, n_tile), n_tile)
            u_all[pl.ds(pl.multiple_of(place[p] * pair, 16), pair), at] = jnp.dot(
                across_t, cots[:, at], preferred_element_type=F32
            )
            return c

        lax.fori_loop(0, kv // n_tile, body, 0)

    def sg_part(p, r):
        w = w_all[pl.ds(pl.multiple_of(place[p] * pair, 16), pair)]
        return lax.dot_general(
            cots[r], w, (((1,), (1,)), ((), ())), preferred_element_type=F32
        )

    def sg_theirs(p):
        sg_send[p] = sg_part(p, pl.ds(tok, tok)).astype(BF16)
        sg_cross[p].start()

    def sg_ours(p):
        sg_mine[p] = sg_part(p, pl.ds(0, tok))

    def keys_half(first, out, kind):
        def body(n, c):
            at = pl.ds(pl.multiple_of(n * n_tile, n_tile), n_tile)
            total = jnp.zeros((tok, n_tile), F32)
            for p in range(PAIRS):
                total = total + jnp.dot(
                    x_mine[p, pl.ds(first, tok)],
                    w_all[pl.ds(pl.multiple_of(place[p] * pair, 16), pair), at],
                    preferred_element_type=F32,
                )
            out[:, at] = total.astype(kind)
            return c

        lax.fori_loop(0, kv // n_tile, body, 0)

    def scatter(way, k):
        return pltpu.make_async_remote_copy(
            src_ref=rs_send.at[way, k], dst_ref=rs_recv.at[way, k], send_sem=rs_ss.at[way, k],
            recv_sem=rs_rs.at[way, k], device_id=ring_to(way), device_id_type=MESH,
        )

    rs = [[scatter(way, k) for k in range(STEPS)] for way in (0, 1)]

    def scatter_send(k):
        for way in (0, 1):
            distance, h = SCATTER[way][k]
            b = block_rows(way, distance, h, True)
            if k >= 2:
                rs[way][k - 2].wait_recv()

            def body(t, c, way=way, b=b, k=k):
                r = pl.ds(pl.multiple_of(t * 32, 32), 32)
                term = u_all[pl.ds(pl.multiple_of(b.start + t * 32, 32), 32)]
                if k >= 2:
                    term = term + rs_recv[way, k - 2, r].astype(F32)
                rs_send[way, k, r] = term.astype(BF16)
                return c

            lax.fori_loop(0, half // 32, body, 0)
            rs[way][k].start()

    gather_step(2)
    x_cross[1].start()
    pg_second.wait_recv()
    pg_s2[...] = pg_s1[...] + pg_b[...]

    @pl.when(core == 1)
    def _():
        pg_third.start()

    gather_step(3)
    x_cross[0].start()
    gather_step(4)
    x_cross[3].wait_recv()
    cots_cross.wait_recv()
    u_pair(3)
    scatter_send(0)
    x_cross[2].wait_recv()
    u_pair(2)
    scatter_send(1)
    sg_theirs(0)
    gather_step(5)
    sg_theirs(1)

    @pl.when(core == 0)
    def _():
        pg_third.wait_recv()
        pg_third.start()

    x_cross[1].wait_recv()
    u_pair(1)
    gather_step(6)
    sg_theirs(2)
    scatter_send(2)
    sg_theirs(3)
    x_cross[0].wait_recv()
    u_pair(0)
    scatter_send(3)

    @pl.when(core == 1)
    def _():
        pg_third.wait_recv()

    pg_total[rows_of(y)] = pg_s2[...] + pg_c[...]
    for c in pg_last:
        c.start()
    keys_half(tok, k_send, BF16)
    k_cross.start()
    sg_ours(0)
    scatter_send(4)
    sg_ours(1)
    sg_ours(2)
    scatter_send(5)
    sg_ours(3)
    scatter_send(6)
    keys_half(0, k_mine, F32)
    for c in pg_last:
        c.wait_recv()

    for p in (0, 1, 2, 3):
        sg_cross[p].wait_recv()

    def finish_rows(t, c):
        r = pl.ds(pl.multiple_of(t * 16, 16), 16)
        total = jnp.zeros((16, pair), F32)
        for p in range(PAIRS):
            total = total + sg_mine[p, r] * x_mine[p, r].astype(F32)
            total = total + sg_recv[p, r].astype(F32) * x_other[p, r].astype(F32)
        i = inv[r]
        m = jnp.sum(total, axis=1, keepdims=True) * (1.0 / width) * i * i
        for p in range(PAIRS):
            ig_buf[r, col(xhi * mid + place[p] * pair)] = (sg_mine[p, r] - m * x_mine[p, r].astype(F32)).astype(BF16)
            ig_buf[r, col((1 - xhi) * mid + place[p] * pair)] = (
                sg_recv[p, r].astype(F32) - m * x_other[p, r].astype(F32)
            ).astype(BF16)
        return c

    lax.fori_loop(0, tok // 16, finish_rows, 0)

    k_cross.wait_recv()

    def finish_keys(t, c):
        r = pl.ds(pl.multiple_of(t * 32, 32), 32)
        k_buf[r] = ((k_mine[r] + k_recv[r].astype(F32)) * (inv[r] * (width ** -0.5))).astype(BF16)
        return c

    lax.fori_loop(0, tok // 32, finish_keys, 0)

    for k in (5, 6):
        for way in (0, 1):
            rs[way][k].wait_recv()
    gain_sum = []
    for h in (0, 1):
        k_up, k_down = (6, 5) if h == 0 else (5, 6)

        def body(t, c, h=h, k_up=k_up, k_down=k_down):
            r = pl.ds(pl.multiple_of(t * 32, 32), 32)
            rr = pl.ds(pl.multiple_of(h * half + t * 32, 32), 32)
            total = u_all[pl.ds(pl.multiple_of(base + h * half + t * 32, 32), 32)]
            total = total + rs_recv[0, k_up, r].astype(F32) + rs_recv[1, k_down, r].astype(F32)
            wg_buf[rr] = (total * gain_col[rr]).astype(BF16)
            weighted[rr] = jnp.sum(total * lw[rr].astype(F32), axis=1, keepdims=True)
            return c

        lax.fori_loop(0, half // 32, body, 0)
    gg_out[...] = to_row(weighted[...], rows)

    for way in (0, 1):
        for k in range(STEPS):
            ag[way][k].wait_send()
            rs[way][k].wait_send()
    for c in cnt + x_cross + sg_cross + pg_first + pg_last + [cots_cross, k_cross, pg_second, pg_third]:
        c.wait_send()


def finish(
    keys, ig, wg, gg, total, outer, moment, frag,
    keys_out, ig_out, wg_out, gg_out, no_out, nm_out,
    o, m, new_o, new_m, sem,
):
    rows, cols = o.shape
    at = pl.ds(pl.multiple_of(frag[0] * cols, cols), cols)
    copies = [
        pltpu.make_async_copy(outer.at[:, at], o, sem.at[0]),
        pltpu.make_async_copy(moment.at[:, at], m, sem.at[1]),
        pltpu.make_async_copy(ig, ig_out, sem.at[2]),
        pltpu.make_async_copy(keys, keys_out, sem.at[3]),
        pltpu.make_async_copy(wg, wg_out, sem.at[4]),
        pltpu.make_async_copy(gg, gg_out, sem.at[5]),
    ]
    for c in copies:
        c.start()
    copies[0].wait()
    copies[1].wait()
    pseudo = o[...] - total[...] * (1.0 / 16)
    new_m[...] = OUTER_MU * m[...] + pseudo
    new_o[...] = o[...] - OUTER_LR * (pseudo + OUTER_MU * new_m[...])
    last = [
        pltpu.make_async_copy(new_o, no_out, sem.at[6]),
        pltpu.make_async_copy(new_m, nm_out, sem.at[7]),
    ]
    for c in last:
        c.start()
    for c in copies[2:] + last:
        c.wait()


def local(
    inputs, key_grad, seg_ids, advantages, gains, local_weights, outer_weights, momentum, frag_index
):
    tok, width = inputs.shape[1:]
    kv, rows = key_grad.shape[2], local_weights.shape[1]
    half, pair, cols = rows // 2, 2 * rows, kv // NFRAG
    hbm, vmem = pl.BlockSpec(memory_space=pltpu.HBM), pl.BlockSpec(memory_space=pltpu.VMEM)
    smem = pl.BlockSpec(memory_space=pltpu.SMEM)
    dma = pltpu.SemaphoreType.DMA
    scratch = [
        pltpu.VMEM((PAIRS, 2 * tok, pair), BF16),
        pltpu.VMEM((PAIRS, tok, pair), BF16),
        pltpu.VMEM((RING * rows, kv), BF16),
        pltpu.VMEM((2 * tok, kv), BF16),
        pltpu.VMEM((tok, kv), BF16),
        pltpu.VMEM((rows, kv), BF16),
        pltpu.VMEM((tok, 1), F32),
        pltpu.VMEM((rows, 1), F32),
        pltpu.VMEM((tok, 1), F32),
        pltpu.VMEM((RING * rows, kv), F32),
        pltpu.VMEM((2, STEPS, half, kv), BF16),
        pltpu.VMEM((2, STEPS, half, kv), BF16),
        pltpu.VMEM((PAIRS, tok, pair), F32),
        pltpu.VMEM((PAIRS, tok, pair), BF16),
        pltpu.VMEM((PAIRS, tok, pair), BF16),
        pltpu.VMEM((tok, kv), F32),
        pltpu.VMEM((tok, kv), BF16),
        pltpu.VMEM((tok, kv), BF16),
        pltpu.VMEM((2, 8, 128), F32),
        pltpu.VMEM((RING, 8, 128), F32),
        pltpu.VMEM((rows, cols), BF16),
        pltpu.VMEM((4, rows // 4, cols), BF16),
        pltpu.VMEM((rows // 4, cols), F32),
        pltpu.VMEM((rows // 4, cols), F32),
        pltpu.VMEM((rows // 4, cols), F32),
        pltpu.VMEM((rows // 4, cols), F32),
        dma((10,)), dma((2, STEPS)), dma((2, STEPS)), dma((2, STEPS)), dma((2, STEPS)),
        dma((10,)), dma((10,)), dma((RING,)), dma((RING,)), dma((9,)), dma((9,)),
    ]
    flops = 6 * 2 * tok * (width // 2) * kv
    keys, input_grad, weight_grad, gain_grad, total = pl.pallas_call(
        kernel,
        out_shape=[
            pltpu.VMEM((tok, kv), BF16),
            pltpu.VMEM((tok, width), BF16),
            pltpu.VMEM((rows, kv), BF16),
            pltpu.VMEM((1, rows), F32),
            pltpu.VMEM((rows, cols), F32),
        ],
        in_specs=[hbm, hbm, vmem, vmem, vmem, hbm, smem],
        out_specs=[vmem] * 5,
        scratch_shapes=scratch,
        compiler_params=pltpu.CompilerParams(
            collective_id=0, has_side_effects=True, vmem_limit_bytes=52 * 2**20
        ),
        cost_estimate=pl.CostEstimate(
            flops=10 * flops, bytes_accessed=200 * 2**20, transcendentals=0
        ),
        name="key_projection",
    )(inputs[0], key_grad[0], seg_ids, advantages, gains, local_weights[0], frag_index)
    keys, input_grad, weight_grad, gain_grad, new_outer, new_momentum = pl.pallas_call(
        finish,
        out_shape=[
            jax.ShapeDtypeStruct((tok, kv), BF16),
            jax.ShapeDtypeStruct((tok, width), BF16),
            jax.ShapeDtypeStruct((rows, kv), BF16),
            jax.ShapeDtypeStruct((1, rows), F32),
            jax.ShapeDtypeStruct((rows, cols), F32),
            jax.ShapeDtypeStruct((rows, cols), F32),
        ],
        in_specs=[vmem] * 5 + [hbm, hbm, smem],
        out_specs=[hbm] * 6,
        scratch_shapes=[pltpu.VMEM((rows, cols), F32)] * 4 + [dma((8,))],
        compiler_params=pltpu.CompilerParams(vmem_limit_bytes=16 * 2**20),
        name="finish",
    )(keys, input_grad, weight_grad, gain_grad, total, outer_weights, momentum, frag_index)
    return keys[None], input_grad[None], weight_grad[None], gain_grad, new_outer, new_momentum


def solution(mesh):
    in_specs = (
        P("group", "fsdp", None),
        P("group", "fsdp", None),
        P("group", "fsdp"),
        P("group", None),
        P("group", "fsdp"),
        P("group", "fsdp", None),
        P("fsdp", None),
        P("fsdp", None),
        P(),
    )
    out_specs = (
        P("group", "fsdp", None),
        P("group", "fsdp", None),
        P("group", "fsdp", None),
        P("group", "fsdp"),
        P("fsdp", None),
        P("fsdp", None),
    )
    return jax.shard_map(local, mesh=mesh, in_specs=in_specs, out_specs=out_specs, check_vma=False)
```

```python
import functools

import jax
import jax.numpy as jnp
from jax import lax
from jax.experimental import pallas as pl
from jax.experimental.pallas import tpu as pltpu
from jax.sharding import PartitionSpec as P

MESH = pl.DeviceIdType.MESH
F32 = jnp.float32
BF16 = jnp.bfloat16
EPSILON = 1e-06
OUTER_MU = 0.9
OUTER_LR = 0.7
NFRAG = 4
RING = 8
PAIRS = 4
STEPS = 7

GATHER = (
    ((0, 0), (0, 1), (1, 0), (1, 1), (2, 0), (2, 1), (3, 0)),
    ((0, 1), (0, 0), (1, 1), (1, 0), (2, 1), (2, 0), (3, 1)),
)
SCATTER = (
    ((4, 0), (3, 1), (3, 0), (2, 1), (2, 0), (1, 1), (1, 0)),
    ((4, 1), (3, 0), (3, 1), (2, 0), (2, 1), (1, 0), (1, 1)),
)


def to_column(row, n):
    here = lax.broadcasted_iota(jnp.int32, (n, n), 0) == lax.broadcasted_iota(jnp.int32, (n, n), 1)
    return jnp.sum(jnp.where(here, jnp.broadcast_to(row, (n, n)), 0.0), axis=1, keepdims=True)


def to_row(column, n):
    here = lax.broadcasted_iota(jnp.int32, (n, n), 0) == lax.broadcasted_iota(jnp.int32, (n, n), 1)
    return jnp.sum(jnp.where(here, jnp.broadcast_to(column, (n, n)), 0.0), axis=0, keepdims=True)


def kernel(
    inputs, key_grad, seg, adv, gains, weights, frag,
    k_buf, ig_buf, wg_buf, gg_out, pg_total,
    x_mine, x_other, w_all, cots, kg, lw, inv, gain_col, weighted,
    u_all, rs_send, rs_recv, sg_mine, sg_send, sg_recv, k_mine, k_send, k_recv,
    cnt_own, cnt_recv, pg_own, pg_a, pg_s1, pg_b, pg_s2, pg_c,
    load_sem, ag_ss, ag_rs, rs_ss, rs_rs, x_ss, x_rs, cnt_ss, cnt_rs, pg_ss, pg_rs,
):
    tok, width = inputs.shape
    kv = key_grad.shape[1]
    rows = weights.shape[0]
    half = rows // 2
    pair = 2 * rows
    mid = width // 2
    cols = kv // NFRAG
    quarter = rows // 4
    seqs = adv.shape[1]

    g, f = lax.axis_index("group"), lax.axis_index("fsdp")
    xhi, z = f // RING, lax.rem(f, RING)
    par = lax.rem(z, 2)
    up = xhi * RING + lax.rem(z + 1, RING)
    down = xhi * RING + lax.rem(z + RING - 1, RING)
    across = (1 - xhi) * RING + z
    core, y = lax.rem(g, 2), g // 4
    side = g + 2 - 4 * lax.rem(g // 2, 2)
    other_core = g + 1 - 2 * core
    over_y = [lax.rem(g + 4 * i, 16) for i in (1, 2, 3)]
    j = z // 2
    place = (j, lax.rem(j + 3 + 2 * par, 4), lax.rem(j + 1 + 2 * par, 4), lax.rem(j + 2, 4))

    def load(src, dst, i):
        c = pltpu.make_async_copy(src, dst, load_sem.at[i])
        c.start()
        return c

    def col(start):
        return pl.ds(pl.multiple_of(start, 128), pair)

    lw_load = load(weights, lw, 0)

    barrier = pltpu.get_barrier_semaphore()
    ring = [xhi * RING + lax.rem(z + i, RING) for i in range(1, RING)]
    for peer in ring + [across]:
        pl.semaphore_signal(barrier, inc=1, device_id={"fsdp": peer}, device_id_type=MESH)
    for peer in over_y + [side]:
        pl.semaphore_signal(barrier, inc=1, device_id={"group": peer}, device_id_type=MESH)

    @pl.when(core == 0)
    def _():
        pl.semaphore_signal(barrier, inc=1, device_id={"group": other_core}, device_id_type=MESH)

    gain_col[...] = to_column(gains[...].astype(F32), rows)
    lw_load.wait()
    base = z * rows

    def scale_rows(t, c):
        r = pl.ds(pl.multiple_of(t * 32, 32), 32)
        w_all[pl.ds(pl.multiple_of(base + t * 32, 32), 32)] = (
            lw[r].astype(F32) * gain_col[r]
        ).astype(BF16)
        return c

    lax.fori_loop(0, rows // 32, scale_rows, 0)
    pl.semaphore_wait(barrier, RING + 4 + core)

    def ring_to(way):
        return {"fsdp": up if way == 0 else down}

    def block_rows(way, distance, h, outward):
        sign = 1 if (way == 0) == outward else -1
        b = lax.rem(z + sign * distance + RING, RING)
        return pl.ds(pl.multiple_of(b * rows + h * half, 16), half)

    def gather(way, k):
        distance, h = GATHER[way][k]
        r = block_rows(way, distance, h, False)
        return pltpu.make_async_remote_copy(
            src_ref=w_all.at[r], dst_ref=w_all.at[r], send_sem=ag_ss.at[way, k],
            recv_sem=ag_rs.at[way, k], device_id=ring_to(way), device_id_type=MESH,
        )

    ag = [[gather(way, k) for k in range(STEPS)] for way in (0, 1)]

    def gather_start(k):
        for way in (0, 1):
            ag[way][k].start()

    def gather_step(k):
        for way in (0, 1):
            ag[way][k].wait_recv()
            if k + 2 < STEPS:
                ag[way][k + 2].start()

    def cross(src, dst, i):
        return pltpu.make_async_remote_copy(
            src_ref=src, dst_ref=dst, send_sem=x_ss.at[i], recv_sem=x_rs.at[i],
            device_id={"fsdp": across}, device_id_type=MESH,
        )

    x_cross = [
        cross(inputs.at[:, col((1 - xhi) * mid + place[p] * pair)], x_mine.at[p, pl.ds(tok, tok)], p)
        for p in range(PAIRS)
    ]
    cots_cross = cross(cots.at[pl.ds(0, tok)], cots.at[pl.ds(tok, tok)], 4)
    sg_cross = [cross(sg_send.at[p], sg_recv.at[p], 5 + p) for p in range(PAIRS)]
    k_cross = [
        cross(k_send.at[pl.ds(h * half, half)], k_recv.at[pl.ds(h * half, half)], 9 + h) for h in (0, 1)
    ]

    gather_start(0)
    x_cross[3].start()
    gather_start(1)
    x_loads = []
    for p in range(PAIRS):
        x_loads.append(load(inputs.at[:, col(xhi * mid + place[p] * pair)], x_mine.at[p, pl.ds(0, tok)], 1 + p))
        x_loads.append(load(inputs.at[:, col((1 - xhi) * mid + place[p] * pair)], x_other.at[p], 5 + p))
    kg_load = load(key_grad, kg, 9)

    seg_col = to_column(seg[...].astype(F32), tok)
    lane = lax.broadcasted_iota(jnp.int32, (tok, 128), 1).astype(F32)
    onehot = jnp.where(jnp.broadcast_to(seg_col, (tok, 128)) == lane, 1.0, 0.0)
    counts = jnp.sum(onehot, axis=0, keepdims=True)
    cnt_own[0] = jnp.broadcast_to(counts, (8, 128))

    def count_copy(src, dst, i, peer):
        c = pltpu.make_async_remote_copy(
            src_ref=src, dst_ref=dst, send_sem=cnt_ss.at[i], recv_sem=cnt_rs.at[i],
            device_id={"fsdp": peer}, device_id_type=MESH,
        )
        c.start()
        return c

    cnt = [count_copy(cnt_own.at[0], cnt_recv.at[0], 0, across)]
    x_cross[2].start()

    chosen = frag[0]

    def pick_rows(t, c):
        r = pl.ds(pl.multiple_of(t * 32, 32), 32)
        out = lw[r, pl.ds(0, cols)].astype(F32)
        for i in range(1, NFRAG):
            out = jnp.where(chosen == i, lw[r, pl.ds(i * cols, cols)].astype(F32), out)
        pg_own[r] = out.astype(BF16)
        return c

    def to_group(src, dst, i, peer):
        return pltpu.make_async_remote_copy(
            src_ref=src, dst_ref=dst, send_sem=pg_ss.at[i], recv_sem=pg_rs.at[i],
            device_id={"group": peer}, device_id_type=MESH,
        )

    def rows_of(yy):
        return pl.ds(pl.multiple_of(yy * quarter, 16), quarter)

    pg_first = [
        to_group(pg_own.at[rows_of(lax.rem(y + i, 4))], pg_a.at[i], i, over_y[i - 1]) for i in (1, 2, 3)
    ]
    pg_second = to_group(pg_s1, pg_b, 4, side)
    pg_third = to_group(pg_s2, pg_c, 5, other_core)
    pg_last = [
        to_group(pg_total.at[rows_of(y)], pg_total.at[rows_of(y)], 5 + i, over_y[i - 1])
        for i in (1, 2, 3)
    ]


    def mean_square(t, c):
        r = pl.ds(pl.multiple_of(t * 16, 16), 16)
        total = jnp.zeros((16, pair), F32)
        for p in range(PAIRS):
            a, b = x_mine[p, r].astype(F32), x_other[p, r].astype(F32)
            total = total + a * a + b * b
        inv[r] = lax.rsqrt(jnp.sum(total, axis=1, keepdims=True) * (1.0 / width) + EPSILON)
        return c


    cnt[0].wait_recv()
    cnt_own[1] = cnt_own[0] + cnt_recv[0]
    for i in range(1, RING):
        cnt.append(count_copy(cnt_own.at[1], cnt_recv.at[i], i, ring[i - 1]))
    for c in x_loads:
        c.wait()
    lax.fori_loop(0, tok // 16, mean_square, 0)
    gather_step(0)
    lax.fori_loop(0, rows // 32, pick_rows, 0)
    for c in pg_first:
        c.start()
    lengths = cnt_own[1, pl.ds(0, 1), :]
    for i in range(1, RING):
        cnt[i].wait_recv()
        lengths = lengths + cnt_recv[i, pl.ds(0, 1), :]

    group_tokens = tok * 2 * RING
    per_seq = (
        adv[...] * (group_tokens / seqs)
        / jnp.maximum(lengths[:, :seqs], group_tokens / (2 * seqs))
    )
    token_weight = jnp.sum(onehot[:, :seqs] * per_seq, axis=1, keepdims=True)
    weighted[...] = token_weight * inv[...] * (width ** -0.5)
    kg_load.wait()

    def scale_tokens(t, c):
        r = pl.ds(pl.multiple_of(t * 32, 32), 32)
        cots[r] = (kg[r].astype(F32) * weighted[r]).astype(BF16)
        return c

    lax.fori_loop(0, tok // 32, scale_tokens, 0)
    cots_cross.start()
    gather_step(1)

    n_tile = 256

    def u_pair(p):
        across_t = x_mine[p].T

        def body(n, c):
            at = pl.ds(pl.multiple_of(n * n_tile, n_tile), n_tile)
            u_all[pl.ds(pl.multiple_of(place[p] * pair, 16), pair), at] = jnp.dot(
                across_t, cots[:, at], preferred_element_type=F32
            )
            return c

        lax.fori_loop(0, kv // n_tile, body, 0)

    def sg_part(p, r):
        w = w_all[pl.ds(pl.multiple_of(place[p] * pair, 16), pair)]
        return lax.dot_general(
            cots[r], w, (((1,), (1,)), ((), ())), preferred_element_type=F32
        )

    def sg_theirs(p):
        sg_send[p] = sg_part(p, pl.ds(tok, tok)).astype(BF16)
        sg_cross[p].start()

    def sg_ours(p):
        sg_mine[p] = sg_part(p, pl.ds(0, tok))

    def keys_half(first, out, kind):
        def body(n, c):
            at = pl.ds(pl.multiple_of(n * n_tile, n_tile), n_tile)
            total = jnp.zeros((tok, n_tile), F32)
            for p in range(PAIRS):
                total = total + jnp.dot(
                    x_mine[p, pl.ds(first, tok)],
                    w_all[pl.ds(pl.multiple_of(place[p] * pair, 16), pair), at],
                    preferred_element_type=F32,
                )
            out[:, at] = total.astype(kind)
            return c

        lax.fori_loop(0, kv // n_tile, body, 0)

    def scatter(way, k):
        return pltpu.make_async_remote_copy(
            src_ref=rs_send.at[way, k], dst_ref=rs_recv.at[way, k], send_sem=rs_ss.at[way, k],
            recv_sem=rs_rs.at[way, k], device_id=ring_to(way), device_id_type=MESH,
        )

    rs = [[scatter(way, k) for k in range(STEPS)] for way in (0, 1)]

    def scatter_send(k):
        for way in (0, 1):
            distance, h = SCATTER[way][k]
            b = block_rows(way, distance, h, True)
            if k >= 2:
                rs[way][k - 2].wait_recv()

            def body(t, c, way=way, b=b, k=k):
                r = pl.ds(pl.multiple_of(t * 32, 32), 32)
                term = u_all[pl.ds(pl.multiple_of(b.start + t * 32, 32), 32)]
                if k >= 2:
                    term = term + rs_recv[way, k - 2, r].astype(F32)
                rs_send[way, k, r] = term.astype(BF16)
                return c

            lax.fori_loop(0, half // 32, body, 0)
            rs[way][k].start()

    for c in pg_first:
        c.wait_recv()
    pg_s1[...] = (
        pg_own[rows_of(y)].astype(F32) + pg_a[1].astype(F32) + pg_a[2].astype(F32)
        + pg_a[3].astype(F32)
    )
    pg_second.start()
    gather_step(2)
    x_cross[1].start()
    pg_second.wait_recv()
    pg_s2[...] = pg_s1[...] + pg_b[...]

    @pl.when(core == 1)
    def _():
        pg_third.start()

    gather_step(3)
    x_cross[0].start()
    gather_step(4)
    x_cross[3].wait_recv()
    cots_cross.wait_recv()
    u_pair(3)
    scatter_send(0)
    x_cross[2].wait_recv()
    u_pair(2)
    scatter_send(1)
    sg_theirs(0)
    gather_step(5)
    sg_theirs(1)

    @pl.when(core == 0)
    def _():
        pg_third.wait_recv()
        pg_third.start()

    x_cross[1].wait_recv()
    u_pair(1)
    gather_step(6)
    sg_theirs(2)
    scatter_send(2)
    sg_theirs(3)
    x_cross[0].wait_recv()
    u_pair(0)
    scatter_send(3)

    @pl.when(core == 1)
    def _():
        pg_third.wait_recv()

    pg_total[rows_of(y)] = pg_s2[...] + pg_c[...]
    for c in pg_last:
        c.start()
    keys_half(tok, k_send, BF16)
    for c in k_cross:
        c.start()
    sg_ours(0)
    scatter_send(4)
    sg_ours(1)
    sg_ours(2)
    scatter_send(5)
    sg_ours(3)
    scatter_send(6)
    keys_half(0, k_mine, F32)
    for c in pg_last:
        c.wait_recv()

    for way in (0, 1):
        for k in range(STEPS):
            ag[way][k].wait_send()
    for c in cnt + x_cross + pg_first + pg_last + [cots_cross, pg_second, pg_third]:
        c.wait_send()

    for p in (0, 1, 2, 3):
        sg_cross[p].wait_recv()

    def finish_rows(t, c):
        r = pl.ds(pl.multiple_of(t * 16, 16), 16)
        total = jnp.zeros((16, pair), F32)
        for p in range(PAIRS):
            total = total + sg_mine[p, r] * x_mine[p, r].astype(F32)
            total = total + sg_recv[p, r].astype(F32) * x_other[p, r].astype(F32)
        i = inv[r]
        m = jnp.sum(total, axis=1, keepdims=True) * (1.0 / width) * i * i
        for p in range(PAIRS):
            ig_buf[r, col(xhi * mid + place[p] * pair)] = (sg_mine[p, r] - m * x_mine[p, r].astype(F32)).astype(BF16)
            ig_buf[r, col((1 - xhi) * mid + place[p] * pair)] = (
                sg_recv[p, r].astype(F32) - m * x_other[p, r].astype(F32)
            ).astype(BF16)
        return c

    lax.fori_loop(0, tok // 16, finish_rows, 0)

    def add_own(h, way, k):
        rs[way][k].wait_recv()

        def body(t, c):
            r = pl.ds(pl.multiple_of(t * 32, 32), 32)
            rr = pl.ds(pl.multiple_of(base + h * half + t * 32, 32), 32)
            u_all[rr] = u_all[rr] + rs_recv[way, k, r].astype(F32)
            return c

        lax.fori_loop(0, half // 32, body, 0)

    add_own(1, 0, 5)
    add_own(0, 1, 5)
    for way in (0, 1):
        for k in range(STEPS - 1):
            rs[way][k].wait_send()
    for c in sg_cross:
        c.wait_send()

    def finish_keys(h):
        k_cross[h].wait_recv()

        def body(t, c):
            r = pl.ds(pl.multiple_of(h * half + t * 32, 32), 32)
            k_buf[r] = ((k_mine[r] + k_recv[r].astype(F32)) * (inv[r] * (width ** -0.5))).astype(BF16)
            return c

        lax.fori_loop(0, half // 32, body, 0)

    finish_keys(0)

    for way in (0, 1):
        rs[way][6].wait_recv()

        def body(t, c, way=way):
            r = pl.ds(pl.multiple_of(t * 32, 32), 32)
            rr = pl.ds(pl.multiple_of(way * half + t * 32, 32), 32)
            total = u_all[pl.ds(pl.multiple_of(base + way * half + t * 32, 32), 32)]
            total = total + rs_recv[way, 6, r].astype(F32)
            wg_buf[rr] = (total * gain_col[rr]).astype(BF16)
            weighted[rr] = jnp.sum(total * lw[rr].astype(F32), axis=1, keepdims=True)
            return c

        lax.fori_loop(0, half // 32, body, 0)
    gg_out[...] = to_row(weighted[...], rows)
    finish_keys(1)

    for c in k_cross + [rs[0][6], rs[1][6]]:
        c.wait_send()


def finish(
    keys, ig, wg, gg, total, outer, moment, frag,
    keys_out, ig_out, wg_out, gg_out, no_out, nm_out,
    o, m, new_o, new_m, sem,
):
    rows, cols = o.shape
    at = pl.ds(pl.multiple_of(frag[0] * cols, cols), cols)
    copies = [
        pltpu.make_async_copy(outer.at[:, at], o, sem.at[0]),
        pltpu.make_async_copy(moment.at[:, at], m, sem.at[1]),
        pltpu.make_async_copy(ig, ig_out, sem.at[2]),
        pltpu.make_async_copy(keys, keys_out, sem.at[3]),
        pltpu.make_async_copy(wg, wg_out, sem.at[4]),
        pltpu.make_async_copy(gg, gg_out, sem.at[5]),
    ]
    for c in copies:
        c.start()
    copies[0].wait()
    copies[1].wait()
    pseudo = o[...] - total[...] * (1.0 / 16)
    new_m[...] = OUTER_MU * m[...] + pseudo
    new_o[...] = o[...] - OUTER_LR * (pseudo + OUTER_MU * new_m[...])
    last = [
        pltpu.make_async_copy(new_o, no_out, sem.at[6]),
        pltpu.make_async_copy(new_m, nm_out, sem.at[7]),
    ]
    for c in last:
        c.start()
    for c in copies[2:] + last:
        c.wait()


def local(
    inputs, key_grad, seg_ids, advantages, gains, local_weights, outer_weights, momentum, frag_index
):
    tok, width = inputs.shape[1:]
    kv, rows = key_grad.shape[2], local_weights.shape[1]
    half, pair, cols = rows // 2, 2 * rows, kv // NFRAG
    hbm, vmem = pl.BlockSpec(memory_space=pltpu.HBM), pl.BlockSpec(memory_space=pltpu.VMEM)
    smem = pl.BlockSpec(memory_space=pltpu.SMEM)
    dma = pltpu.SemaphoreType.DMA
    scratch = [
        pltpu.VMEM((PAIRS, 2 * tok, pair), BF16),
        pltpu.VMEM((PAIRS, tok, pair), BF16),
        pltpu.VMEM((RING * rows, kv), BF16),
        pltpu.VMEM((2 * tok, kv), BF16),
        pltpu.VMEM((tok, kv), BF16),
        pltpu.VMEM((rows, kv), BF16),
        pltpu.VMEM((tok, 1), F32),
        pltpu.VMEM((rows, 1), F32),
        pltpu.VMEM((tok, 1), F32),
        pltpu.VMEM((RING * rows, kv), F32),
        pltpu.VMEM((2, STEPS, half, kv), BF16),
        pltpu.VMEM((2, STEPS, half, kv), BF16),
        pltpu.VMEM((PAIRS, tok, pair), F32),
        pltpu.VMEM((PAIRS, tok, pair), BF16),
        pltpu.VMEM((PAIRS, tok, pair), BF16),
        pltpu.VMEM((tok, kv), F32),
        pltpu.VMEM((tok, kv), BF16),
        pltpu.VMEM((tok, kv), BF16),
        pltpu.VMEM((2, 8, 128), F32),
        pltpu.VMEM((RING, 8, 128), F32),
        pltpu.VMEM((rows, cols), BF16),
        pltpu.VMEM((4, rows // 4, cols), BF16),
        pltpu.VMEM((rows // 4, cols), F32),
        pltpu.VMEM((rows // 4, cols), F32),
        pltpu.VMEM((rows // 4, cols), F32),
        pltpu.VMEM((rows // 4, cols), F32),
        dma((10,)), dma((2, STEPS)), dma((2, STEPS)), dma((2, STEPS)), dma((2, STEPS)),
        dma((11,)), dma((11,)), dma((RING,)), dma((RING,)), dma((9,)), dma((9,)),
    ]
    flops = 6 * 2 * tok * (width // 2) * kv
    keys, input_grad, weight_grad, gain_grad, total = pl.pallas_call(
        kernel,
        out_shape=[
            pltpu.VMEM((tok, kv), BF16),
            pltpu.VMEM((tok, width), BF16),
            pltpu.VMEM((rows, kv), BF16),
            pltpu.VMEM((1, rows), F32),
            pltpu.VMEM((rows, cols), F32),
        ],
        in_specs=[hbm, hbm, vmem, vmem, vmem, hbm, smem],
        out_specs=[vmem] * 5,
        scratch_shapes=scratch,
        compiler_params=pltpu.CompilerParams(
            collective_id=0, has_side_effects=True, vmem_limit_bytes=52 * 2**20
        ),
        cost_estimate=pl.CostEstimate(
            flops=10 * flops, bytes_accessed=200 * 2**20, transcendentals=0
        ),
        name="key_projection",
    )(inputs[0], key_grad[0], seg_ids, advantages, gains, local_weights[0], frag_index)
    keys, input_grad, weight_grad, gain_grad, new_outer, new_momentum = pl.pallas_call(
        finish,
        out_shape=[
            jax.ShapeDtypeStruct((tok, kv), BF16),
            jax.ShapeDtypeStruct((tok, width), BF16),
            jax.ShapeDtypeStruct((rows, kv), BF16),
            jax.ShapeDtypeStruct((1, rows), F32),
            jax.ShapeDtypeStruct((rows, cols), F32),
            jax.ShapeDtypeStruct((rows, cols), F32),
        ],
        in_specs=[vmem] * 5 + [hbm, hbm, smem],
        out_specs=[hbm] * 6,
        scratch_shapes=[pltpu.VMEM((rows, cols), F32)] * 4 + [dma((8,))],
        compiler_params=pltpu.CompilerParams(vmem_limit_bytes=16 * 2**20),
        name="finish",
    )(keys, input_grad, weight_grad, gain_grad, total, outer_weights, momentum, frag_index)
    return keys[None], input_grad[None], weight_grad[None], gain_grad, new_outer, new_momentum


def solution(mesh):
    in_specs = (
        P("group", "fsdp", None),
        P("group", "fsdp", None),
        P("group", "fsdp"),
        P("group", None),
        P("group", "fsdp"),
        P("group", "fsdp", None),
        P("fsdp", None),
        P("fsdp", None),
        P(),
    )
    out_specs = (
        P("group", "fsdp", None),
        P("group", "fsdp", None),
        P("group", "fsdp", None),
        P("group", "fsdp"),
        P("fsdp", None),
        P("fsdp", None),
    )
    return jax.shard_map(local, mesh=mesh, in_specs=in_specs, out_specs=out_specs, check_vma=False)
```

```python
import functools

import jax
import jax.numpy as jnp
from jax import lax
from jax.experimental import pallas as pl
from jax.experimental.pallas import tpu as pltpu
from jax.sharding import PartitionSpec as P

MESH = pl.DeviceIdType.MESH
F32 = jnp.float32
BF16 = jnp.bfloat16
EPSILON = 1e-06
OUTER_MU = 0.9
OUTER_LR = 0.7
NFRAG = 4
RING = 8
PAIRS = 4
STEPS = 7

GATHER = (
    ((0, 0), (0, 1), (1, 0), (1, 1), (2, 0), (2, 1), (3, 0)),
    ((0, 1), (0, 0), (1, 1), (1, 0), (2, 1), (2, 0), (3, 1)),
)
SCATTER = (
    ((4, 0), (3, 1), (3, 0), (2, 1), (2, 0), (1, 1), (1, 0)),
    ((4, 1), (3, 0), (3, 1), (2, 0), (2, 1), (1, 0), (1, 1)),
)


def to_column(row, n):
    here = lax.broadcasted_iota(jnp.int32, (n, n), 0) == lax.broadcasted_iota(jnp.int32, (n, n), 1)
    return jnp.sum(jnp.where(here, jnp.broadcast_to(row, (n, n)), 0.0), axis=1, keepdims=True)


def to_row(column, n):
    here = lax.broadcasted_iota(jnp.int32, (n, n), 0) == lax.broadcasted_iota(jnp.int32, (n, n), 1)
    return jnp.sum(jnp.where(here, jnp.broadcast_to(column, (n, n)), 0.0), axis=0, keepdims=True)


def kernel(
    inputs, key_grad, seg_in, adv_in, gains_in, weights, frag,
    k_buf, ig_buf, wg_buf, gg_out, pg_total,
    x_mine, x_other, w_all, cots, kg, lw, inv, gain_col, weighted,
    seg, adv, gains, u_all, rs_send, rs_recv, sg_mine, sg_send, sg_recv, k_mine, k_send, k_recv,
    cnt_own, cnt_recv, pg_own, pg_a, pg_s1, pg_b, pg_s2, pg_c,
    load_sem, ag_ss, ag_rs, rs_ss, rs_rs, x_ss, x_rs, cnt_ss, cnt_rs, pg_ss, pg_rs,
):
    tok, width = inputs.shape
    kv = key_grad.shape[1]
    rows = weights.shape[0]
    half = rows // 2
    pair = 2 * rows
    mid = width // 2
    cols = kv // NFRAG
    quarter = rows // 4
    seqs = adv_in.shape[1]

    g, f = lax.axis_index("group"), lax.axis_index("fsdp")
    xhi, z = f // RING, lax.rem(f, RING)
    par = lax.rem(z, 2)
    up = xhi * RING + lax.rem(z + 1, RING)
    down = xhi * RING + lax.rem(z + RING - 1, RING)
    across = (1 - xhi) * RING + z
    core, y = lax.rem(g, 2), g // 4
    side = g + 2 - 4 * lax.rem(g // 2, 2)
    other_core = g + 1 - 2 * core
    over_y = [lax.rem(g + 4 * i, 16) for i in (1, 2, 3)]
    j = z // 2
    place = (j, lax.rem(j + 3 + 2 * par, 4), lax.rem(j + 1 + 2 * par, 4), lax.rem(j + 2, 4))

    def load(src, dst, i):
        c = pltpu.make_async_copy(src, dst, load_sem.at[i])
        c.start()
        return c

    def col(start):
        return pl.ds(pl.multiple_of(start, 128), pair)

    gain_load = load(gains_in, gains, 10)
    lw_load = load(weights, lw, 0)
    seg_load = load(seg_in, seg, 11)
    adv_load = load(adv_in, adv, 12)

    barrier = pltpu.get_barrier_semaphore()
    ring = [xhi * RING + lax.rem(z + i, RING) for i in range(1, RING)]
    for peer in ring + [across]:
        pl.semaphore_signal(barrier, inc=1, device_id={"fsdp": peer}, device_id_type=MESH)
    for peer in over_y + [side]:
        pl.semaphore_signal(barrier, inc=1, device_id={"group": peer}, device_id_type=MESH)

    @pl.when(core == 0)
    def _():
        pl.semaphore_signal(barrier, inc=1, device_id={"group": other_core}, device_id_type=MESH)

    gain_load.wait()
    gain_col[...] = to_column(gains[...].astype(F32), rows)
    lw_load.wait()
    base = z * rows

    def scale_rows(t, c):
        r = pl.ds(pl.multiple_of(t * 32, 32), 32)
        w_all[pl.ds(pl.multiple_of(base + t * 32, 32), 32)] = (
            lw[r].astype(F32) * gain_col[r]
        ).astype(BF16)
        return c

    lax.fori_loop(0, rows // 32, scale_rows, 0)
    pl.semaphore_wait(barrier, RING + 4 + core)

    def ring_to(way):
        return {"fsdp": up if way == 0 else down}

    def block_rows(way, distance, h, outward):
        sign = 1 if (way == 0) == outward else -1
        b = lax.rem(z + sign * distance + RING, RING)
        return pl.ds(pl.multiple_of(b * rows + h * half, 16), half)

    def gather(way, k):
        distance, h = GATHER[way][k]
        r = block_rows(way, distance, h, False)
        return pltpu.make_async_remote_copy(
            src_ref=w_all.at[r], dst_ref=w_all.at[r], send_sem=ag_ss.at[way, k],
            recv_sem=ag_rs.at[way, k], device_id=ring_to(way), device_id_type=MESH,
        )

    ag = [[gather(way, k) for k in range(STEPS)] for way in (0, 1)]

    def gather_start(k):
        for way in (0, 1):
            ag[way][k].start()

    def gather_step(k):
        for way in (0, 1):
            ag[way][k].wait_recv()
            if k + 2 < STEPS:
                ag[way][k + 2].start()

    def cross(src, dst, i):
        return pltpu.make_async_remote_copy(
            src_ref=src, dst_ref=dst, send_sem=x_ss.at[i], recv_sem=x_rs.at[i],
            device_id={"fsdp": across}, device_id_type=MESH,
        )

    x_cross = [
        cross(inputs.at[:, col((1 - xhi) * mid + place[p] * pair)], x_mine.at[p, pl.ds(tok, tok)], p)
        for p in range(PAIRS)
    ]
    cots_cross = cross(cots.at[pl.ds(0, tok)], cots.at[pl.ds(tok, tok)], 4)
    sg_cross = [cross(sg_send.at[p], sg_recv.at[p], 5 + p) for p in range(PAIRS)]
    k_cross = [
        cross(k_send.at[pl.ds(h * half, half)], k_recv.at[pl.ds(h * half, half)], 9 + h) for h in (0, 1)
    ]

    gather_start(0)
    x_cross[3].start()
    gather_start(1)
    x_loads = []
    for p in range(PAIRS):
        x_loads.append(load(inputs.at[:, col(xhi * mid + place[p] * pair)], x_mine.at[p, pl.ds(0, tok)], 1 + p))
        x_loads.append(load(inputs.at[:, col((1 - xhi) * mid + place[p] * pair)], x_other.at[p], 5 + p))
    kg_load = load(key_grad, kg, 9)

    seg_load.wait()
    seg_col = to_column(seg[...].astype(F32), tok)
    lane = lax.broadcasted_iota(jnp.int32, (tok, 128), 1).astype(F32)
    onehot = jnp.where(jnp.broadcast_to(seg_col, (tok, 128)) == lane, 1.0, 0.0)
    counts = jnp.sum(onehot, axis=0, keepdims=True)
    cnt_own[0] = jnp.broadcast_to(counts, (8, 128))

    def count_copy(src, dst, i, peer):
        c = pltpu.make_async_remote_copy(
            src_ref=src, dst_ref=dst, send_sem=cnt_ss.at[i], recv_sem=cnt_rs.at[i],
            device_id={"fsdp": peer}, device_id_type=MESH,
        )
        c.start()
        return c

    cnt = [count_copy(cnt_own.at[0], cnt_recv.at[0], 0, across)]
    x_cross[2].start()

    chosen = frag[0]

    def pick_rows(t, c):
        r = pl.ds(pl.multiple_of(t * 32, 32), 32)
        out = lw[r, pl.ds(0, cols)].astype(F32)
        for i in range(1, NFRAG):
            out = jnp.where(chosen == i, lw[r, pl.ds(i * cols, cols)].astype(F32), out)
        pg_own[r] = out.astype(BF16)
        return c

    def to_group(src, dst, i, peer):
        return pltpu.make_async_remote_copy(
            src_ref=src, dst_ref=dst, send_sem=pg_ss.at[i], recv_sem=pg_rs.at[i],
            device_id={"group": peer}, device_id_type=MESH,
        )

    def rows_of(yy):
        return pl.ds(pl.multiple_of(yy * quarter, 16), quarter)

    pg_first = [
        to_group(pg_own.at[rows_of(lax.rem(y + i, 4))], pg_a.at[i], i, over_y[i - 1]) for i in (1, 2, 3)
    ]
    pg_second = to_group(pg_s1, pg_b, 4, side)
    pg_third = to_group(pg_s2, pg_c, 5, other_core)
    pg_last = [
        to_group(pg_total.at[rows_of(y)], pg_total.at[rows_of(y)], 5 + i, over_y[i - 1])
        for i in (1, 2, 3)
    ]


    def mean_square(t, c):
        r = pl.ds(pl.multiple_of(t * 16, 16), 16)
        total = jnp.zeros((16, pair), F32)
        for p in range(PAIRS):
            a, b = x_mine[p, r].astype(F32), x_other[p, r].astype(F32)
            total = total + a * a + b * b
        inv[r] = lax.rsqrt(jnp.sum(total, axis=1, keepdims=True) * (1.0 / width) + EPSILON)
        return c


    cnt[0].wait_recv()
    cnt_own[1] = cnt_own[0] + cnt_recv[0]
    for i in range(1, RING):
        cnt.append(count_copy(cnt_own.at[1], cnt_recv.at[i], i, ring[i - 1]))
    for c in x_loads:
        c.wait()
    lax.fori_loop(0, tok // 16, mean_square, 0)
    gather_step(0)
    lax.fori_loop(0, rows // 32, pick_rows, 0)
    for c in pg_first:
        c.start()
    lengths = cnt_own[1, pl.ds(0, 1), :]
    for i in range(1, RING):
        cnt[i].wait_recv()
        lengths = lengths + cnt_recv[i, pl.ds(0, 1), :]

    adv_load.wait()
    group_tokens = tok * 2 * RING
    per_seq = (
        adv[...] * (group_tokens / seqs)
        / jnp.maximum(lengths[:, :seqs], group_tokens / (2 * seqs))
    )
    token_weight = jnp.sum(onehot[:, :seqs] * per_seq, axis=1, keepdims=True)
    weighted[...] = token_weight * inv[...] * (width ** -0.5)
    kg_load.wait()

    def scale_tokens(t, c):
        r = pl.ds(pl.multiple_of(t * 32, 32), 32)
        cots[r] = (kg[r].astype(F32) * weighted[r]).astype(BF16)
        return c

    lax.fori_loop(0, tok // 32, scale_tokens, 0)
    cots_cross.start()
    gather_step(1)

    n_tile = 256

    def u_pair(p):
        across_t = x_mine[p].T

        def body(n, c):
            at = pl.ds(pl.multiple_of(n * n_tile, n_tile), n_tile)
            u_all[pl.ds(pl.multiple_of(place[p] * pair, 16), pair), at] = jnp.dot(
                across_t, cots[:, at], preferred_element_type=F32
            )
            return c

        lax.fori_loop(0, kv // n_tile, body, 0)

    def sg_part(p, r):
        w = w_all[pl.ds(pl.multiple_of(place[p] * pair, 16), pair)]
        return lax.dot_general(
            cots[r], w, (((1,), (1,)), ((), ())), preferred_element_type=F32
        )

    def sg_theirs(p):
        sg_send[p] = sg_part(p, pl.ds(tok, tok)).astype(BF16)
        sg_cross[p].start()

    def sg_ours(p):
        sg_mine[p] = sg_part(p, pl.ds(0, tok))

    def keys_half(first, out, kind):
        def body(n, c):
            at = pl.ds(pl.multiple_of(n * n_tile, n_tile), n_tile)
            total = jnp.zeros((tok, n_tile), F32)
            for p in range(PAIRS):
                total = total + jnp.dot(
                    x_mine[p, pl.ds(first, tok)],
                    w_all[pl.ds(pl.multiple_of(place[p] * pair, 16), pair), at],
                    preferred_element_type=F32,
                )
            out[:, at] = total.astype(kind)
            return c

        lax.fori_loop(0, kv // n_tile, body, 0)

    def scatter(way, k):
        return pltpu.make_async_remote_copy(
            src_ref=rs_send.at[way, k], dst_ref=rs_recv.at[way, k], send_sem=rs_ss.at[way, k],
            recv_sem=rs_rs.at[way, k], device_id=ring_to(way), device_id_type=MESH,
        )

    rs = [[scatter(way, k) for k in range(STEPS)] for way in (0, 1)]

    def scatter_send(k):
        for way in (0, 1):
            distance, h = SCATTER[way][k]
            b = block_rows(way, distance, h, True)
            if k >= 2:
                rs[way][k - 2].wait_recv()

            def body(t, c, way=way, b=b, k=k):
                r = pl.ds(pl.multiple_of(t * 32, 32), 32)
                term = u_all[pl.ds(pl.multiple_of(b.start + t * 32, 32), 32)]
                if k >= 2:
                    term = term + rs_recv[way, k - 2, r].astype(F32)
                rs_send[way, k, r] = term.astype(BF16)
                return c

            lax.fori_loop(0, half // 32, body, 0)
            rs[way][k].start()

    for c in pg_first:
        c.wait_recv()
    pg_s1[...] = (
        pg_own[rows_of(y)].astype(F32) + pg_a[1].astype(F32) + pg_a[2].astype(F32)
        + pg_a[3].astype(F32)
    )
    pg_second.start()
    gather_step(2)
    x_cross[1].start()
    pg_second.wait_recv()
    pg_s2[...] = pg_s1[...] + pg_b[...]

    @pl.when(core == 1)
    def _():
        pg_third.start()

    gather_step(3)
    x_cross[0].start()
    gather_step(4)
    x_cross[3].wait_recv()
    cots_cross.wait_recv()
    u_pair(3)
    scatter_send(0)
    x_cross[2].wait_recv()
    u_pair(2)
    scatter_send(1)
    sg_theirs(0)
    gather_step(5)
    sg_theirs(1)

    @pl.when(core == 0)
    def _():
        pg_third.wait_recv()
        pg_third.start()

    x_cross[1].wait_recv()
    u_pair(1)
    gather_step(6)
    sg_theirs(2)
    scatter_send(2)
    sg_theirs(3)
    x_cross[0].wait_recv()
    u_pair(0)
    scatter_send(3)

    @pl.when(core == 1)
    def _():
        pg_third.wait_recv()

    pg_total[rows_of(y)] = pg_s2[...] + pg_c[...]
    for c in pg_last:
        c.start()
    keys_half(tok, k_send, BF16)
    for c in k_cross:
        c.start()
    sg_ours(0)
    scatter_send(4)
    sg_ours(1)
    sg_ours(2)
    scatter_send(5)
    sg_ours(3)
    scatter_send(6)
    keys_half(0, k_mine, F32)
    for c in pg_last:
        c.wait_recv()

    for way in (0, 1):
        for k in range(STEPS):
            ag[way][k].wait_send()
    for c in cnt + x_cross + pg_first + pg_last + [cots_cross, pg_second, pg_third]:
        c.wait_send()

    for p in (0, 1, 2, 3):
        sg_cross[p].wait_recv()

    def finish_rows(t, c):
        r = pl.ds(pl.multiple_of(t * 16, 16), 16)
        total = jnp.zeros((16, pair), F32)
        for p in range(PAIRS):
            total = total + sg_mine[p, r] * x_mine[p, r].astype(F32)
            total = total + sg_recv[p, r].astype(F32) * x_other[p, r].astype(F32)
        i = inv[r]
        m = jnp.sum(total, axis=1, keepdims=True) * (1.0 / width) * i * i
        for p in range(PAIRS):
            ig_buf[r, col(xhi * mid + place[p] * pair)] = (sg_mine[p, r] - m * x_mine[p, r].astype(F32)).astype(BF16)
            ig_buf[r, col((1 - xhi) * mid + place[p] * pair)] = (
                sg_recv[p, r].astype(F32) - m * x_other[p, r].astype(F32)
            ).astype(BF16)
        return c

    lax.fori_loop(0, tok // 16, finish_rows, 0)

    def add_own(h, way, k):
        rs[way][k].wait_recv()

        def body(t, c):
            r = pl.ds(pl.multiple_of(t * 32, 32), 32)
            rr = pl.ds(pl.multiple_of(base + h * half + t * 32, 32), 32)
            u_all[rr] = u_all[rr] + rs_recv[way, k, r].astype(F32)
            return c

        lax.fori_loop(0, half // 32, body, 0)

    add_own(1, 0, 5)
    add_own(0, 1, 5)
    for way in (0, 1):
        for k in range(STEPS - 1):
            rs[way][k].wait_send()
    for c in sg_cross:
        c.wait_send()

    def finish_keys(h):
        k_cross[h].wait_recv()

        def body(t, c):
            r = pl.ds(pl.multiple_of(h * half + t * 32, 32), 32)
            k_buf[r] = ((k_mine[r] + k_recv[r].astype(F32)) * (inv[r] * (width ** -0.5))).astype(BF16)
            return c

        lax.fori_loop(0, half // 32, body, 0)

    finish_keys(0)

    for way in (0, 1):
        rs[way][6].wait_recv()

        def body(t, c, way=way):
            r = pl.ds(pl.multiple_of(t * 32, 32), 32)
            rr = pl.ds(pl.multiple_of(way * half + t * 32, 32), 32)
            total = u_all[pl.ds(pl.multiple_of(base + way * half + t * 32, 32), 32)]
            total = total + rs_recv[way, 6, r].astype(F32)
            wg_buf[rr] = (total * gain_col[rr]).astype(BF16)
            weighted[rr] = jnp.sum(total * lw[rr].astype(F32), axis=1, keepdims=True)
            return c

        lax.fori_loop(0, half // 32, body, 0)
    gg_out[...] = to_row(weighted[...], rows)
    finish_keys(1)

    for c in k_cross + [rs[0][6], rs[1][6]]:
        c.wait_send()


def finish(
    keys, ig, wg, gg, total, outer, moment, frag,
    keys_out, ig_out, wg_out, gg_out, no_out, nm_out,
    new_o, new_m, sem,
):
    rows, cols = new_o.shape
    tok = ig.shape[0]
    part = tok // 4
    at = pl.ds(pl.multiple_of(frag[0] * cols, cols), cols)
    copies = [
        pltpu.make_async_copy(
            ig.at[pl.ds(i * part, part)], ig_out.at[pl.ds(i * part, part)], sem.at[i]
        )
        for i in range(4)
    ] + [
        pltpu.make_async_copy(keys, keys_out, sem.at[4]),
        pltpu.make_async_copy(wg, wg_out, sem.at[5]),
        pltpu.make_async_copy(gg, gg_out, sem.at[6]),
    ]
    for c in copies:
        c.start()
    o, m = outer[:, at], moment[:, at]
    pseudo = o - total[...] * (1.0 / 16)
    new_m[...] = OUTER_MU * m + pseudo
    new_o[...] = o - OUTER_LR * (pseudo + OUTER_MU * new_m[...])
    last = [
        pltpu.make_async_copy(new_o, no_out, sem.at[7]),
        pltpu.make_async_copy(new_m, nm_out, sem.at[8]),
    ]
    for c in last:
        c.start()
    for c in copies + last:
        c.wait()


def local(
    inputs, key_grad, seg_ids, advantages, gains, local_weights, outer_weights, momentum, frag_index
):
    tok, width = inputs.shape[1:]
    kv, rows = key_grad.shape[2], local_weights.shape[1]
    half, pair, cols = rows // 2, 2 * rows, kv // NFRAG
    hbm, vmem = pl.BlockSpec(memory_space=pltpu.HBM), pl.BlockSpec(memory_space=pltpu.VMEM)
    smem = pl.BlockSpec(memory_space=pltpu.SMEM)
    dma = pltpu.SemaphoreType.DMA
    scratch = [
        pltpu.VMEM((PAIRS, 2 * tok, pair), BF16),
        pltpu.VMEM((PAIRS, tok, pair), BF16),
        pltpu.VMEM((RING * rows, kv), BF16),
        pltpu.VMEM((2 * tok, kv), BF16),
        pltpu.VMEM((tok, kv), BF16),
        pltpu.VMEM((rows, kv), BF16),
        pltpu.VMEM((tok, 1), F32),
        pltpu.VMEM((rows, 1), F32),
        pltpu.VMEM((tok, 1), F32),
        pltpu.VMEM(seg_ids.shape, seg_ids.dtype),
        pltpu.VMEM(advantages.shape, F32),
        pltpu.VMEM(gains.shape, gains.dtype),
        pltpu.VMEM((RING * rows, kv), F32),
        pltpu.VMEM((2, STEPS, half, kv), BF16),
        pltpu.VMEM((2, STEPS, half, kv), BF16),
        pltpu.VMEM((PAIRS, tok, pair), F32),
        pltpu.VMEM((PAIRS, tok, pair), BF16),
        pltpu.VMEM((PAIRS, tok, pair), BF16),
        pltpu.VMEM((tok, kv), F32),
        pltpu.VMEM((tok, kv), BF16),
        pltpu.VMEM((tok, kv), BF16),
        pltpu.VMEM((2, 8, 128), F32),
        pltpu.VMEM((RING, 8, 128), F32),
        pltpu.VMEM((rows, cols), BF16),
        pltpu.VMEM((4, rows // 4, cols), BF16),
        pltpu.VMEM((rows // 4, cols), F32),
        pltpu.VMEM((rows // 4, cols), F32),
        pltpu.VMEM((rows // 4, cols), F32),
        pltpu.VMEM((rows // 4, cols), F32),
        dma((13,)), dma((2, STEPS)), dma((2, STEPS)), dma((2, STEPS)), dma((2, STEPS)),
        dma((11,)), dma((11,)), dma((RING,)), dma((RING,)), dma((9,)), dma((9,)),
    ]
    flops = 6 * 2 * tok * (width // 2) * kv
    keys, input_grad, weight_grad, gain_grad, total = pl.pallas_call(
        kernel,
        out_shape=[
            pltpu.VMEM((tok, kv), BF16),
            pltpu.VMEM((tok, width), BF16),
            pltpu.VMEM((rows, kv), BF16),
            pltpu.VMEM((1, rows), F32),
            pltpu.VMEM((rows, cols), F32),
        ],
        in_specs=[hbm] * 6 + [smem],
        out_specs=[vmem] * 5,
        scratch_shapes=scratch,
        compiler_params=pltpu.CompilerParams(
            collective_id=0, has_side_effects=True, vmem_limit_bytes=52 * 2**20
        ),
        cost_estimate=pl.CostEstimate(
            flops=10 * flops, bytes_accessed=200 * 2**20, transcendentals=0
        ),
        name="key_projection",
    )(inputs[0], key_grad[0], seg_ids, advantages, gains, local_weights[0], frag_index)
    keys, input_grad, weight_grad, gain_grad, new_outer, new_momentum = pl.pallas_call(
        finish,
        out_shape=[
            jax.ShapeDtypeStruct((tok, kv), BF16),
            jax.ShapeDtypeStruct((tok, width), BF16),
            jax.ShapeDtypeStruct((rows, kv), BF16),
            jax.ShapeDtypeStruct((1, rows), F32),
            jax.ShapeDtypeStruct((rows, cols), F32),
            jax.ShapeDtypeStruct((rows, cols), F32),
        ],
        in_specs=[vmem] * 7 + [smem],
        out_specs=[hbm] * 6,
        scratch_shapes=[pltpu.VMEM((rows, cols), F32)] * 2 + [dma((9,))],
        compiler_params=pltpu.CompilerParams(vmem_limit_bytes=16 * 2**20),
        name="finish",
    )(keys, input_grad, weight_grad, gain_grad, total, outer_weights, momentum, frag_index)
    return keys[None], input_grad[None], weight_grad[None], gain_grad, new_outer, new_momentum


def solution(mesh):
    in_specs = (
        P("group", "fsdp", None),
        P("group", "fsdp", None),
        P("group", "fsdp"),
        P("group", None),
        P("group", "fsdp"),
        P("group", "fsdp", None),
        P("fsdp", None),
        P("fsdp", None),
        P(),
    )
    out_specs = (
        P("group", "fsdp", None),
        P("group", "fsdp", None),
        P("group", "fsdp", None),
        P("group", "fsdp"),
        P("fsdp", None),
        P("fsdp", None),
    )
    return jax.shard_map(local, mesh=mesh, in_specs=in_specs, out_specs=out_specs, check_vma=False)
```

```python
import functools

import jax
import jax.numpy as jnp
from jax import lax
from jax.experimental import pallas as pl
from jax.experimental.pallas import tpu as pltpu
from jax.sharding import PartitionSpec as P

MESH = pl.DeviceIdType.MESH
F32 = jnp.float32
BF16 = jnp.bfloat16
EPSILON = 1e-06
OUTER_MU = 0.9
OUTER_LR = 0.7
NFRAG = 4
RING = 8
PAIRS = 4
STEPS = 7

GATHER = (
    ((0, 0), (0, 1), (1, 0), (1, 1), (2, 0), (2, 1), (3, 0)),
    ((0, 1), (0, 0), (1, 1), (1, 0), (2, 1), (2, 0), (3, 1)),
)
SCATTER = (
    ((4, 0), (3, 1), (3, 0), (2, 1), (2, 0), (1, 1), (1, 0)),
    ((4, 1), (3, 0), (3, 1), (2, 0), (2, 1), (1, 0), (1, 1)),
)


def to_column(row, n):
    here = lax.broadcasted_iota(jnp.int32, (n, n), 0) == lax.broadcasted_iota(jnp.int32, (n, n), 1)
    return jnp.sum(jnp.where(here, jnp.broadcast_to(row, (n, n)), 0.0), axis=1, keepdims=True)


def to_row(column, n):
    here = lax.broadcasted_iota(jnp.int32, (n, n), 0) == lax.broadcasted_iota(jnp.int32, (n, n), 1)
    return jnp.sum(jnp.where(here, jnp.broadcast_to(column, (n, n)), 0.0), axis=0, keepdims=True)


def kernel(
    inputs, key_grad, seg_in, adv_in, gains_in, weights, frag,
    k_buf, ig_buf, wg_buf, gg_out, pg_total,
    x_mine, x_other, w_all, cots, kg, lw, inv, gain_col, weighted,
    seg, adv, gains, u_all, rs_send, rs_recv, sg_mine, sg_send, sg_recv, k_mine, k_send, k_recv,
    cnt_own, cnt_recv, pg_own, pg_a, pg_s1, pg_b, pg_s2, pg_c,
    load_sem, ag_ss, ag_rs, rs_ss, rs_rs, x_ss, x_rs, cnt_ss, cnt_rs, pg_ss, pg_rs,
):
    tok, width = inputs.shape
    kv = key_grad.shape[1]
    rows = weights.shape[0]
    half = rows // 2
    pair = 2 * rows
    mid = width // 2
    cols = kv // NFRAG
    quarter = rows // 4
    seqs = adv_in.shape[1]

    g, f = lax.axis_index("group"), lax.axis_index("fsdp")
    xhi, z = f // RING, lax.rem(f, RING)
    par = lax.rem(z, 2)
    up = xhi * RING + lax.rem(z + 1, RING)
    down = xhi * RING + lax.rem(z + RING - 1, RING)
    across = (1 - xhi) * RING + z
    core, y = lax.rem(g, 2), g // 4
    side = g + 2 - 4 * lax.rem(g // 2, 2)
    other_core = g + 1 - 2 * core
    over_y = [lax.rem(g + 4 * i, 16) for i in (1, 2, 3)]
    j = z // 2
    place = (j, lax.rem(j + 3 + 2 * par, 4), lax.rem(j + 1 + 2 * par, 4), lax.rem(j + 2, 4))

    def load(src, dst, i):
        c = pltpu.make_async_copy(src, dst, load_sem.at[i])
        c.start()
        return c

    def col(start):
        return pl.ds(pl.multiple_of(start, 128), pair)

    gain_load = load(gains_in, gains, 10)
    lw_load = load(weights, lw, 0)
    seg_load = load(seg_in, seg, 11)
    adv_load = load(adv_in, adv, 12)

    barrier = pltpu.get_barrier_semaphore()
    ring = [xhi * RING + lax.rem(z + i, RING) for i in range(1, RING)]
    for peer in ring + [across]:
        pl.semaphore_signal(barrier, inc=1, device_id={"fsdp": peer}, device_id_type=MESH)
    for peer in over_y + [side]:
        pl.semaphore_signal(barrier, inc=1, device_id={"group": peer}, device_id_type=MESH)

    @pl.when(core == 0)
    def _():
        pl.semaphore_signal(barrier, inc=1, device_id={"group": other_core}, device_id_type=MESH)

    gain_load.wait()
    gain_col[...] = to_column(gains[...].astype(F32), rows)
    seg_load.wait()
    seg_col = to_column(seg[...].astype(F32), tok)
    lane = lax.broadcasted_iota(jnp.int32, (tok, 128), 1).astype(F32)
    onehot = jnp.where(jnp.broadcast_to(seg_col, (tok, 128)) == lane, 1.0, 0.0)
    counts = jnp.sum(onehot, axis=0, keepdims=True)
    cnt_own[0] = jnp.broadcast_to(counts, (8, 128))
    lw_load.wait()
    base = z * rows

    def scale_rows(t, c):
        r = pl.ds(pl.multiple_of(t * 32, 32), 32)
        w_all[pl.ds(pl.multiple_of(base + t * 32, 32), 32)] = (
            lw[r].astype(F32) * gain_col[r]
        ).astype(BF16)
        return c

    lax.fori_loop(0, rows // 32, scale_rows, 0)
    pl.semaphore_wait(barrier, RING + 4 + core)

    def count_copy(src, dst, i, peer):
        c = pltpu.make_async_remote_copy(
            src_ref=src, dst_ref=dst, send_sem=cnt_ss.at[i], recv_sem=cnt_rs.at[i],
            device_id={"fsdp": peer}, device_id_type=MESH,
        )
        c.start()
        return c

    cnt = [count_copy(cnt_own.at[0], cnt_recv.at[0], 0, across)]

    def ring_to(way):
        return {"fsdp": up if way == 0 else down}

    def block_rows(way, distance, h, outward):
        sign = 1 if (way == 0) == outward else -1
        b = lax.rem(z + sign * distance + RING, RING)
        return pl.ds(pl.multiple_of(b * rows + h * half, 16), half)

    def gather(way, k):
        distance, h = GATHER[way][k]
        r = block_rows(way, distance, h, False)
        return pltpu.make_async_remote_copy(
            src_ref=w_all.at[r], dst_ref=w_all.at[r], send_sem=ag_ss.at[way, k],
            recv_sem=ag_rs.at[way, k], device_id=ring_to(way), device_id_type=MESH,
        )

    ag = [[gather(way, k) for k in range(STEPS)] for way in (0, 1)]

    def gather_start(k):
        for way in (0, 1):
            ag[way][k].start()

    def gather_step(k):
        for way in (0, 1):
            ag[way][k].wait_recv()
            if k + 2 < STEPS:
                ag[way][k + 2].start()

    def cross(src, dst, i):
        return pltpu.make_async_remote_copy(
            src_ref=src, dst_ref=dst, send_sem=x_ss.at[i], recv_sem=x_rs.at[i],
            device_id={"fsdp": across}, device_id_type=MESH,
        )

    x_cross = [
        cross(inputs.at[:, col((1 - xhi) * mid + place[p] * pair)], x_mine.at[p, pl.ds(tok, tok)], p)
        for p in range(PAIRS)
    ]
    cots_cross = cross(cots.at[pl.ds(0, tok)], cots.at[pl.ds(tok, tok)], 4)
    sg_cross = [cross(sg_send.at[p], sg_recv.at[p], 5 + p) for p in range(PAIRS)]
    k_cross = [
        cross(k_send.at[pl.ds(h * half, half)], k_recv.at[pl.ds(h * half, half)], 9 + h) for h in (0, 1)
    ]

    gather_start(0)
    x_cross[3].start()
    x_loads = []
    for p in range(PAIRS):
        x_loads.append(load(inputs.at[:, col(xhi * mid + place[p] * pair)], x_mine.at[p, pl.ds(0, tok)], 1 + p))
        x_loads.append(load(inputs.at[:, col((1 - xhi) * mid + place[p] * pair)], x_other.at[p], 5 + p))
    kg_load = load(key_grad, kg, 9)


    chosen = frag[0]

    def pick_rows(t, c):
        r = pl.ds(pl.multiple_of(t * 32, 32), 32)
        out = lw[r, pl.ds(0, cols)].astype(F32)
        for i in range(1, NFRAG):
            out = jnp.where(chosen == i, lw[r, pl.ds(i * cols, cols)].astype(F32), out)
        pg_own[r] = out.astype(BF16)
        return c

    def to_group(src, dst, i, peer):
        return pltpu.make_async_remote_copy(
            src_ref=src, dst_ref=dst, send_sem=pg_ss.at[i], recv_sem=pg_rs.at[i],
            device_id={"group": peer}, device_id_type=MESH,
        )

    def rows_of(yy):
        return pl.ds(pl.multiple_of(yy * quarter, 16), quarter)

    pg_first = [
        to_group(pg_own.at[rows_of(lax.rem(y + i, 4))], pg_a.at[i], i, over_y[i - 1]) for i in (1, 2, 3)
    ]
    pg_second = to_group(pg_s1, pg_b, 4, side)
    pg_third = to_group(pg_s2, pg_c, 5, other_core)
    pg_last = [
        to_group(pg_total.at[rows_of(y)], pg_total.at[rows_of(y)], 5 + i, over_y[i - 1])
        for i in (1, 2, 3)
    ]


    def mean_square(t, c):
        r = pl.ds(pl.multiple_of(t * 16, 16), 16)
        total = jnp.zeros((16, pair), F32)
        for p in range(PAIRS):
            a, b = x_mine[p, r].astype(F32), x_other[p, r].astype(F32)
            total = total + a * a + b * b
        inv[r] = lax.rsqrt(jnp.sum(total, axis=1, keepdims=True) * (1.0 / width) + EPSILON)
        return c


    cnt[0].wait_recv()
    cnt_own[1] = cnt_own[0] + cnt_recv[0]
    for i in range(1, RING):
        cnt.append(count_copy(cnt_own.at[1], cnt_recv.at[i], i, ring[i - 1]))
    gather_start(1)
    x_cross[2].start()
    for c in x_loads:
        c.wait()
    lax.fori_loop(0, tok // 16, mean_square, 0)
    gather_step(0)
    lax.fori_loop(0, rows // 32, pick_rows, 0)
    for c in pg_first:
        c.start()
    lengths = cnt_own[1, pl.ds(0, 1), :]
    for i in range(1, RING):
        cnt[i].wait_recv()
        lengths = lengths + cnt_recv[i, pl.ds(0, 1), :]

    adv_load.wait()
    group_tokens = tok * 2 * RING
    per_seq = (
        adv[...] * (group_tokens / seqs)
        / jnp.maximum(lengths[:, :seqs], group_tokens / (2 * seqs))
    )
    token_weight = jnp.sum(onehot[:, :seqs] * per_seq, axis=1, keepdims=True)
    weighted[...] = token_weight * inv[...] * (width ** -0.5)
    kg_load.wait()

    def scale_tokens(t, c):
        r = pl.ds(pl.multiple_of(t * 32, 32), 32)
        cots[r] = (kg[r].astype(F32) * weighted[r]).astype(BF16)
        return c

    lax.fori_loop(0, tok // 32, scale_tokens, 0)
    cots_cross.start()
    gather_step(1)

    n_tile = 256

    def u_pair(p):
        across_t = x_mine[p].T

        def body(n, c):
            at = pl.ds(pl.multiple_of(n * n_tile, n_tile), n_tile)
            u_all[pl.ds(pl.multiple_of(place[p] * pair, 16), pair), at] = jnp.dot(
                across_t, cots[:, at], preferred_element_type=F32
            )
            return c

        lax.fori_loop(0, kv // n_tile, body, 0)

    def sg_part(p, r):
        w = w_all[pl.ds(pl.multiple_of(place[p] * pair, 16), pair)]
        return lax.dot_general(
            cots[r], w, (((1,), (1,)), ((), ())), preferred_element_type=F32
        )

    def sg_theirs(p):
        sg_send[p] = sg_part(p, pl.ds(tok, tok)).astype(BF16)
        sg_cross[p].start()

    def sg_ours(p):
        sg_mine[p] = sg_part(p, pl.ds(0, tok))

    def keys_half(first, out, kind):
        def body(n, c):
            at = pl.ds(pl.multiple_of(n * n_tile, n_tile), n_tile)
            total = jnp.zeros((tok, n_tile), F32)
            for p in range(PAIRS):
                total = total + jnp.dot(
                    x_mine[p, pl.ds(first, tok)],
                    w_all[pl.ds(pl.multiple_of(place[p] * pair, 16), pair), at],
                    preferred_element_type=F32,
                )
            out[:, at] = total.astype(kind)
            return c

        lax.fori_loop(0, kv // n_tile, body, 0)

    def scatter(way, k):
        return pltpu.make_async_remote_copy(
            src_ref=rs_send.at[way, k], dst_ref=rs_recv.at[way, k], send_sem=rs_ss.at[way, k],
            recv_sem=rs_rs.at[way, k], device_id=ring_to(way), device_id_type=MESH,
        )

    rs = [[scatter(way, k) for k in range(STEPS)] for way in (0, 1)]

    def scatter_send(k):
        for way in (0, 1):
            distance, h = SCATTER[way][k]
            b = block_rows(way, distance, h, True)
            if k >= 2:
                rs[way][k - 2].wait_recv()

            def body(t, c, way=way, b=b, k=k):
                r = pl.ds(pl.multiple_of(t * 32, 32), 32)
                term = u_all[pl.ds(pl.multiple_of(b.start + t * 32, 32), 32)]
                if k >= 2:
                    term = term + rs_recv[way, k - 2, r].astype(F32)
                rs_send[way, k, r] = term.astype(BF16)
                return c

            lax.fori_loop(0, half // 32, body, 0)
            rs[way][k].start()

    for c in pg_first:
        c.wait_recv()
    pg_s1[...] = (
        pg_own[rows_of(y)].astype(F32) + pg_a[1].astype(F32) + pg_a[2].astype(F32)
        + pg_a[3].astype(F32)
    )
    pg_second.start()
    gather_step(2)
    x_cross[1].start()
    pg_second.wait_recv()
    pg_s2[...] = pg_s1[...] + pg_b[...]

    @pl.when(core == 1)
    def _():
        pg_third.start()

    gather_step(3)
    x_cross[0].start()
    gather_step(4)
    x_cross[3].wait_recv()
    cots_cross.wait_recv()
    u_pair(3)
    scatter_send(0)
    x_cross[2].wait_recv()
    u_pair(2)
    scatter_send(1)
    sg_theirs(0)
    gather_step(5)
    sg_theirs(1)

    @pl.when(core == 0)
    def _():
        pg_third.wait_recv()
        pg_third.start()

    x_cross[1].wait_recv()
    u_pair(1)
    gather_step(6)
    sg_theirs(2)
    scatter_send(2)
    sg_theirs(3)
    x_cross[0].wait_recv()
    u_pair(0)
    scatter_send(3)

    @pl.when(core == 1)
    def _():
        pg_third.wait_recv()

    pg_total[rows_of(y)] = pg_s2[...] + pg_c[...]
    for c in pg_last:
        c.start()
    keys_half(tok, k_send, BF16)
    for c in k_cross:
        c.start()
    sg_ours(0)
    scatter_send(4)
    sg_ours(1)
    sg_ours(2)
    scatter_send(5)
    sg_ours(3)
    scatter_send(6)
    keys_half(0, k_mine, F32)
    for c in pg_last:
        c.wait_recv()

    for way in (0, 1):
        for k in range(STEPS):
            ag[way][k].wait_send()
    for c in cnt + x_cross + pg_first + pg_last + [cots_cross, pg_second, pg_third]:
        c.wait_send()

    for p in (0, 1, 2, 3):
        sg_cross[p].wait_recv()

    def finish_rows(t, c):
        r = pl.ds(pl.multiple_of(t * 16, 16), 16)
        total = jnp.zeros((16, pair), F32)
        for p in range(PAIRS):
            total = total + sg_mine[p, r] * x_mine[p, r].astype(F32)
            total = total + sg_recv[p, r].astype(F32) * x_other[p, r].astype(F32)
        i = inv[r]
        m = jnp.sum(total, axis=1, keepdims=True) * (1.0 / width) * i * i
        for p in range(PAIRS):
            ig_buf[r, col(xhi * mid + place[p] * pair)] = (sg_mine[p, r] - m * x_mine[p, r].astype(F32)).astype(BF16)
            ig_buf[r, col((1 - xhi) * mid + place[p] * pair)] = (
                sg_recv[p, r].astype(F32) - m * x_other[p, r].astype(F32)
            ).astype(BF16)
        return c

    lax.fori_loop(0, tok // 16, finish_rows, 0)

    def add_own(h, way, k):
        rs[way][k].wait_recv()

        def body(t, c):
            r = pl.ds(pl.multiple_of(t * 32, 32), 32)
            rr = pl.ds(pl.multiple_of(base + h * half + t * 32, 32), 32)
            u_all[rr] = u_all[rr] + rs_recv[way, k, r].astype(F32)
            return c

        lax.fori_loop(0, half // 32, body, 0)

    add_own(1, 0, 5)
    add_own(0, 1, 5)
    for way in (0, 1):
        for k in range(STEPS - 1):
            rs[way][k].wait_send()
    for c in sg_cross:
        c.wait_send()

    def finish_keys(h):
        k_cross[h].wait_recv()

        def body(t, c):
            r = pl.ds(pl.multiple_of(h * half + t * 32, 32), 32)
            k_buf[r] = ((k_mine[r] + k_recv[r].astype(F32)) * (inv[r] * (width ** -0.5))).astype(BF16)
            return c

        lax.fori_loop(0, half // 32, body, 0)

    finish_keys(0)

    for way in (0, 1):
        rs[way][6].wait_recv()

        def body(t, c, way=way):
            r = pl.ds(pl.multiple_of(t * 32, 32), 32)
            rr = pl.ds(pl.multiple_of(way * half + t * 32, 32), 32)
            total = u_all[pl.ds(pl.multiple_of(base + way * half + t * 32, 32), 32)]
            total = total + rs_recv[way, 6, r].astype(F32)
            wg_buf[rr] = (total * gain_col[rr]).astype(BF16)
            weighted[rr] = jnp.sum(total * lw[rr].astype(F32), axis=1, keepdims=True)
            return c

        lax.fori_loop(0, half // 32, body, 0)
    gg_out[...] = to_row(weighted[...], rows)
    finish_keys(1)

    for c in k_cross + [rs[0][6], rs[1][6]]:
        c.wait_send()


def finish(
    keys, ig, wg, gg, total, outer, moment, frag,
    keys_out, ig_out, wg_out, gg_out, no_out, nm_out,
    new_o, new_m, sem,
):
    rows, cols = new_o.shape
    tok = ig.shape[0]
    part = tok // 4
    at = pl.ds(pl.multiple_of(frag[0] * cols, cols), cols)
    copies = [
        pltpu.make_async_copy(
            ig.at[pl.ds(i * part, part)], ig_out.at[pl.ds(i * part, part)], sem.at[i]
        )
        for i in range(4)
    ] + [
        pltpu.make_async_copy(keys, keys_out, sem.at[4]),
        pltpu.make_async_copy(wg, wg_out, sem.at[5]),
        pltpu.make_async_copy(gg, gg_out, sem.at[6]),
    ]
    for c in copies:
        c.start()
    o, m = outer[:, at], moment[:, at]
    pseudo = o - total[...] * (1.0 / 16)
    new_m[...] = OUTER_MU * m + pseudo
    new_o[...] = o - OUTER_LR * (pseudo + OUTER_MU * new_m[...])
    last = [
        pltpu.make_async_copy(new_o, no_out, sem.at[7]),
        pltpu.make_async_copy(new_m, nm_out, sem.at[8]),
    ]
    for c in last:
        c.start()
    for c in copies + last:
        c.wait()


def local(
    inputs, key_grad, seg_ids, advantages, gains, local_weights, outer_weights, momentum, frag_index
):
    tok, width = inputs.shape[1:]
    kv, rows = key_grad.shape[2], local_weights.shape[1]
    half, pair, cols = rows // 2, 2 * rows, kv // NFRAG
    hbm, vmem = pl.BlockSpec(memory_space=pltpu.HBM), pl.BlockSpec(memory_space=pltpu.VMEM)
    smem = pl.BlockSpec(memory_space=pltpu.SMEM)
    dma = pltpu.SemaphoreType.DMA
    scratch = [
        pltpu.VMEM((PAIRS, 2 * tok, pair), BF16),
        pltpu.VMEM((PAIRS, tok, pair), BF16),
        pltpu.VMEM((RING * rows, kv), BF16),
        pltpu.VMEM((2 * tok, kv), BF16),
        pltpu.VMEM((tok, kv), BF16),
        pltpu.VMEM((rows, kv), BF16),
        pltpu.VMEM((tok, 1), F32),
        pltpu.VMEM((rows, 1), F32),
        pltpu.VMEM((tok, 1), F32),
        pltpu.VMEM(seg_ids.shape, seg_ids.dtype),
        pltpu.VMEM(advantages.shape, F32),
        pltpu.VMEM(gains.shape, gains.dtype),
        pltpu.VMEM((RING * rows, kv), F32),
        pltpu.VMEM((2, STEPS, half, kv), BF16),
        pltpu.VMEM((2, STEPS, half, kv), BF16),
        pltpu.VMEM((PAIRS, tok, pair), F32),
        pltpu.VMEM((PAIRS, tok, pair), BF16),
        pltpu.VMEM((PAIRS, tok, pair), BF16),
        pltpu.VMEM((tok, kv), F32),
        pltpu.VMEM((tok, kv), BF16),
        pltpu.VMEM((tok, kv), BF16),
        pltpu.VMEM((2, 8, 128), F32),
        pltpu.VMEM((RING, 8, 128), F32),
        pltpu.VMEM((rows, cols), BF16),
        pltpu.VMEM((4, rows // 4, cols), BF16),
        pltpu.VMEM((rows // 4, cols), F32),
        pltpu.VMEM((rows // 4, cols), F32),
        pltpu.VMEM((rows // 4, cols), F32),
        pltpu.VMEM((rows // 4, cols), F32),
        dma((13,)), dma((2, STEPS)), dma((2, STEPS)), dma((2, STEPS)), dma((2, STEPS)),
        dma((11,)), dma((11,)), dma((RING,)), dma((RING,)), dma((9,)), dma((9,)),
    ]
    flops = 6 * 2 * tok * (width // 2) * kv
    keys, input_grad, weight_grad, gain_grad, total = pl.pallas_call(
        kernel,
        out_shape=[
            pltpu.VMEM((tok, kv), BF16),
            pltpu.VMEM((tok, width), BF16),
            pltpu.VMEM((rows, kv), BF16),
            pltpu.VMEM((1, rows), F32),
            pltpu.VMEM((rows, cols), F32),
        ],
        in_specs=[hbm] * 6 + [smem],
        out_specs=[vmem] * 5,
        scratch_shapes=scratch,
        compiler_params=pltpu.CompilerParams(
            collective_id=0, has_side_effects=True, vmem_limit_bytes=52 * 2**20
        ),
        cost_estimate=pl.CostEstimate(
            flops=10 * flops, bytes_accessed=200 * 2**20, transcendentals=0
        ),
        name="key_projection",
    )(inputs[0], key_grad[0], seg_ids, advantages, gains, local_weights[0], frag_index)
    keys, input_grad, weight_grad, gain_grad, new_outer, new_momentum = pl.pallas_call(
        finish,
        out_shape=[
            jax.ShapeDtypeStruct((tok, kv), BF16),
            jax.ShapeDtypeStruct((tok, width), BF16),
            jax.ShapeDtypeStruct((rows, kv), BF16),
            jax.ShapeDtypeStruct((1, rows), F32),
            jax.ShapeDtypeStruct((rows, cols), F32),
            jax.ShapeDtypeStruct((rows, cols), F32),
        ],
        in_specs=[vmem] * 7 + [smem],
        out_specs=[hbm] * 6,
        scratch_shapes=[pltpu.VMEM((rows, cols), F32)] * 2 + [dma((9,))],
        compiler_params=pltpu.CompilerParams(vmem_limit_bytes=16 * 2**20),
        name="finish",
    )(keys, input_grad, weight_grad, gain_grad, total, outer_weights, momentum, frag_index)
    return keys[None], input_grad[None], weight_grad[None], gain_grad, new_outer, new_momentum


def solution(mesh):
    in_specs = (
        P("group", "fsdp", None),
        P("group", "fsdp", None),
        P("group", "fsdp"),
        P("group", None),
        P("group", "fsdp"),
        P("group", "fsdp", None),
        P("fsdp", None),
        P("fsdp", None),
        P(),
    )
    out_specs = (
        P("group", "fsdp", None),
        P("group", "fsdp", None),
        P("group", "fsdp", None),
        P("group", "fsdp"),
        P("fsdp", None),
        P("fsdp", None),
    )
    return jax.shard_map(local, mesh=mesh, in_specs=in_specs, out_specs=out_specs, check_vma=False)
```
